32 devices in a mesh: band: 4 (over y, x), slab: 8 (over z, core).
Axes of the slice: x: 2, y: 2, z: 4, core: 2. Of those that a mesh axis runs over, the one named last changes fastest.
Arguments:
- psi: bfloat16 [32, 524288], P(('band', 'slab')), may hold values from -6 to 6
- beta: bfloat16 [8, 512, 1152], P('slab', 'band'), may hold values from -0.75 to 0.75
- pair_atom: int32 [8, 512], P('slab'), may hold values from 0 to 128, as said below
- pair_block: int32 [8, 512], P('slab'), may hold values from 0 to 1023
- proj_count: int32 [128], replicated, may hold values from 4 to 18, as said below
- strength: float32 [128, 18, 18], replicated, may hold values from -0.6 to 0.6
Outputs:
- applied: bfloat16 [32, 524288], P(('band', 'slab'))
The draws below stay inside these ranges and needn't reach their ends.
Inputs may be any that keep to these rules, and one draw needn't show every extreme that they name: `pair_atom`: in each slab's 512 slots the used ones come first and the empty ones hold 128; some slab uses all its slots. `proj_count`: each atom has 4, 8, 13 or 18 projectors; some atom has 18.
All inputs are finite; a program needn't handle non-finite values.
Results may differ from the reference program's by a relative error of at most 0.0049.
Values may be sent and summed in bfloat16 or wider, within the bound.
No kernel may reach another device: no remote copies, remote signals or barrier semaphores. Data moves between devices by JAX's collectives and lax.ppermute only.
A program may use at most 192 MiB of HBM per device.

```python
import jax
import jax.numpy as jnp
from jax import lax

BLK_DEV = 1024
PAIR_DEV = 512
ATOMS = 128
NPROJ = 18
BLOCK = 64
NBLK = 8192
BANDS = 32
N_SLAB = 8


def draw_pair_atom(key, part):
    key_live, key_full, key_thin, key_atom = jax.random.split(key, 4)
    halving = jax.random.randint(key_live, (N_SLAB,), 0, 4)
    live_count = jnp.right_shift(jnp.full((N_SLAB,), PAIR_DEV, jnp.int32), halving)
    full_slab = jax.random.randint(key_full, (), 0, N_SLAB)
    thin_slab = (full_slab + 1 + jax.random.randint(key_thin, (), 0, N_SLAB - 1)) % N_SLAB
    live_count = live_count.at[full_slab].set(PAIR_DEV).at[thin_slab].set(PAIR_DEV // 8)
    slot_index = jnp.arange(PAIR_DEV, dtype=jnp.int32)[None, :]
    center = jnp.arange(N_SLAB, dtype=jnp.int32) * ATOMS // N_SLAB + ATOMS // (2 * N_SLAB)
    spread_width = ATOMS // 4
    offset = jax.random.randint(key_atom, (N_SLAB, PAIR_DEV), -spread_width, spread_width + 1)
    atom_index = (center[:, None] + offset) % ATOMS
    return jnp.where(slot_index < live_count[:, None], atom_index, ATOMS).astype(jnp.int32)


def draw_proj_count(key, part):
    key_kind, key_pick = jax.random.split(key)
    kinds = jnp.array([4, 8, 13, NPROJ], jnp.int32)
    chosen = kinds[jax.random.randint(key_kind, (ATOMS,), 0, 4)]
    return chosen.at[jax.random.randint(key_pick, (), 0, ATOMS)].set(NPROJ).astype(jnp.int32)


def with_ends(entries, rng, smallest, largest):
    shape = entries.shape
    spot = [jax.random.randint(jax.random.fold_in(rng, axis), (), 0, shape[axis]) for axis in range(len(shape))]
    entries = entries.at[tuple(spot)].set(smallest)
    longest = shape.index(max(shape))
    spot[longest] = (spot[longest] + 1) % shape[longest]
    return entries.at[tuple(spot)].set(largest)


def levels(rng, shape, cuts, low, top_value):
    factor_of, own = 1.0, jax.random.fold_in(rng, 6)
    for axis_at, shards_of in cuts:
        steps = jnp.exp(jax.random.uniform(jax.random.fold_in(own, axis_at), (shards_of,), jnp.float32, low / len(cuts), top_value / len(cuts)))
        factor_of = factor_of * jnp.repeat(steps, shape[axis_at] // shards_of).reshape([-1 if axis == axis_at else 1 for axis in range(len(shape))])
    return factor_of


def scatter_about(rng, extent, width, bound, pieces=(), kind=jnp.bfloat16):
    drawn = jax.random.normal(rng, extent, jnp.float32) * width
    if len(pieces) > 0:
        drawn = levels(rng, extent, pieces, -0.22, 0.18) * drawn
    return jnp.clip(drawn, min=-bound, max=bound).astype(kind)


def setup_inputs(seed: int = 0) -> dict:
    streams_of = jax.random.split(jax.random.key(seed), 7)
    return {
        "psi": scatter_about(streams_of[0], (BANDS, NBLK * BLOCK), 1.0, 6.0, ((0, 32),)),
        "beta": scatter_about(streams_of[1], (N_SLAB, PAIR_DEV, NPROJ * BLOCK), BLOCK ** -0.5, 0.75, ((0, 8), (1, 4))),
        "pair_atom": draw_pair_atom(jax.random.fold_in(streams_of[6], 71), 0),
        "pair_block": with_ends(jax.random.randint(streams_of[3], (N_SLAB, PAIR_DEV), 0, BLK_DEV), jax.random.fold_in(streams_of[3], 1), 0, BLK_DEV - 1).astype(jnp.int32),
        "proj_count": draw_proj_count(jax.random.fold_in(streams_of[6], 71), 0),
        "strength": scatter_about(streams_of[5], (ATOMS, NPROJ, NPROJ), 0.1, 0.6, (), jnp.float32),
    }


def reference(psi, beta, pair_atom, pair_block, proj_count, strength):
    grid_blocks = psi.reshape(BANDS, N_SLAB, BLK_DEV, BLOCK)
    tables = beta.reshape(N_SLAB, PAIR_DEV, NPROJ, BLOCK)

    def project(coef_total, slab_index):
        slab_psi = jnp.take(grid_blocks, slab_index, axis=1)
        picked = jnp.take(slab_psi, pair_block[slab_index], axis=1).astype(jnp.float32)
        table = jnp.take(tables, slab_index, axis=0).astype(jnp.float32)
        products = jnp.einsum('bkg,kpg->kpb', picked, table)
        summed = jax.ops.segment_sum(products, pair_atom[slab_index], num_segments=ATOMS + 1)
        return coef_total + summed[:ATOMS], None

    coef_total, _ = lax.scan(project, jnp.zeros((ATOMS, NPROJ, BANDS), jnp.float32), jnp.arange(N_SLAB))
    proj_valid = (jnp.arange(NPROJ)[None, :] < proj_count[:, None]).astype(jnp.float32)
    masked = coef_total * proj_valid[:, :, None]
    coupled = jnp.einsum('apq,aqb->apb', strength, masked, precision=lax.Precision.HIGHEST)
    scaled = (coupled * proj_valid[:, :, None]).astype(jnp.bfloat16)
    padded = jnp.concatenate([scaled, jnp.zeros((1, NPROJ, BANDS), jnp.bfloat16)], axis=0)

    def spread(slab_index):
        picked = jnp.take(padded, pair_atom[slab_index], axis=0).astype(jnp.float32)
        table = jnp.take(tables, slab_index, axis=0).astype(jnp.float32)
        products = jnp.einsum('kpg,kpb->kbg', table, picked)
        summed = jax.ops.segment_sum(products, pair_block[slab_index], num_segments=BLK_DEV)
        return summed.transpose(1, 0, 2).astype(jnp.bfloat16)

    slab_outputs = lax.map(spread, jnp.arange(N_SLAB))
    return slab_outputs.transpose(1, 0, 2, 3).reshape(BANDS, NBLK * BLOCK)
```

```python
import functools

import jax
import jax.numpy as jnp
from jax import lax
from jax.experimental import pallas as pl
from jax.experimental.pallas import tpu as pltpu
from jax.sharding import PartitionSpec as P

CORES = 2
LANES = 128
GROUP = 16
F32 = jnp.float32
BF16 = jnp.bfloat16
VMEM_SPEC = pl.BlockSpec(memory_space=pltpu.VMEM)
SMEM_SPEC = pl.BlockSpec(memory_space=pltpu.SMEM)
PARAMS = pltpu.CompilerParams(vmem_limit_bytes=40 * 1024 * 1024)


def dot(a, b, contract=((1,), (0,))):
    return lax.dot_general(a, b, (contract, ((), ())), preferred_element_type=F32)


def two_terms(x):
    high = x.astype(BF16)
    return high, (x - high.astype(F32)).astype(BF16)


def iota(shape, axis):
    return lax.broadcasted_iota(jnp.int32, shape, axis)


def column(row):
    return jnp.transpose(jnp.broadcast_to(row, (LANES, LANES)))


def rows_kernel(place_ref, psi_ref, *out_refs):
    step = pl.program_id(0)
    for index, out_ref in enumerate(out_refs):

        @pl.when(step == index)
        def _(out_ref=out_ref):
            def move(i, carry):
                part = psi_ref[0:1, pl.ds(pl.multiple_of(i * 2048, 2048), 2048)]
                out_ref[pl.ds(pl.multiple_of(i * 16, 16), 16), :] = part.reshape(16, LANES)
                return carry

            lax.fori_loop(0, out_ref.shape[0] // 16, move, 0, unroll=8)


def to_rows(psi, chip, chips):
    points = psi.shape[1] // chips
    rows = points // LANES
    return pl.pallas_call(
        rows_kernel,
        grid_spec=pltpu.PrefetchScalarGridSpec(
            num_scalar_prefetch=1,
            grid=(chips,),
            in_specs=[pl.BlockSpec((1, points), lambda i, chip: (0, lax.rem(chip[0] + i, chips)))],
            out_specs=[pl.BlockSpec((rows, LANES), lambda i, chip: (0, 0))] * chips,
        ),
        out_shape=[jax.ShapeDtypeStruct((rows, LANES), BF16)] * chips,
        compiler_params=PARAMS,
    )(chip.reshape(1), psi)


def project_kernel(bands, projectors, padded, core_ref, atom_refs, block_refs, beta_refs, psi_refs, coef_ref, prods):
    slots = atom_refs[0].shape[1]
    slab_rows = psi_refs[0].shape[0] // CORES
    pair_count = projectors // 2
    wide = 2 * bands * GROUP
    lane = iota((LANES, LANES), 1)
    low = lane < LANES // 2
    source = iota((pair_count * wide, bands * padded), 0) // GROUP
    target = iota((pair_count * wide, bands * padded), 1)
    gather_lanes = (target == lax.rem(source, bands) * padded + source // bands).astype(BF16)
    diagonal = lax.rem(iota((GROUP, wide), 0), GROUP) == lax.rem(iota((GROUP, wide), 1), GROUP)
    coef_ref[...] = jnp.zeros_like(coef_ref)
    for slab in range(CORES):
        place = core_ref[0] if slab == 0 else CORES - 1 - core_ref[0]
        first_row = pl.multiple_of(place * slab_rows, slab_rows)

        def chunk(i, carry, slab=slab, first_row=first_row):
            at = pl.ds(pl.multiple_of(i * LANES, LANES), LANES)
            atoms = atom_refs[slab][0:1, at]
            blocks = column(block_refs[slab][0:1, at])
            wanted = jnp.right_shift(blocks, 1)
            odd = jnp.bitwise_and(blocks, 1) == 1
            hits = jnp.concatenate(
                [(wanted - t * LANES == lane).astype(BF16) for t in range(slab_rows // LANES)], axis=1
            )
            lows, highs = [], []
            for psi_ref in psi_refs:
                picked = dot(hits, psi_ref[pl.ds(first_row, slab_rows), :])
                turned = pltpu.roll(picked, LANES // 2, 1)
                both = jnp.where(low == odd, turned, picked)
                lows.append(jnp.where(low, both, 0.0).astype(BF16))
                highs.append(jnp.where(low, 0.0, both).astype(BF16))
            for group in range(LANES // GROUP):
                own = slice(group * GROUP, (group + 1) * GROUP)
                rows = pl.ds(pl.multiple_of(i * LANES + group * GROUP, GROUP), GROUP)
                values = jnp.concatenate([part[own] for part in lows + highs], axis=0)
                tables = jnp.concatenate(
                    [beta_refs[slab][rows, t * LANES : (t + 1) * LANES] for t in range(pair_count)], axis=0
                )
                crossed = dot(tables, values, ((1,), (1,)))
                for t in range(pair_count):
                    kept = jnp.where(diagonal, crossed[t * GROUP : (t + 1) * GROUP], 0.0)
                    prods[own, t * wide : (t + 1) * wide] = kept
            high, rest = two_terms(prods[...])
            slot_coef = dot(high, gather_lanes) + dot(rest, gather_lanes)
            high, rest = two_terms(slot_coef)
            of_atom = (column(atoms) == lane).astype(BF16)
            summed = dot(high, of_atom, ((0,), (0,))) + dot(rest, of_atom, ((0,), (0,)))
            coef_ref[...] += summed
            return carry

        lax.fori_loop(0, slots // LANES, chunk, 0)


def project(core, atoms, blocks, tables, values, projectors, padded, atom_total):
    bands = len(values)
    pair_count = projectors // 2

    def kernel(core_ref, a0, a1, k0, k1, b0, b1, *rest):
        project_kernel(
            bands, projectors, padded, core_ref, (a0, a1), (k0, k1), (b0, b1), rest[:bands], rest[bands], rest[bands + 1]
        )

    return pl.pallas_call(
        kernel,
        in_specs=[SMEM_SPEC] + [VMEM_SPEC] * (6 + bands),
        out_specs=VMEM_SPEC,
        out_shape=jax.ShapeDtypeStruct((bands * padded, atom_total), F32),
        scratch_shapes=[pltpu.VMEM((LANES, pair_count * 2 * bands * GROUP), F32)],
        compiler_params=PARAMS,
    )(core.reshape(1), *atoms, *blocks, *tables, *values)


def apply_kernel(bands, projectors, padded, atom_refs, beta_refs, count_ref, strength_ref, coef_refs, out_refs, wide_refs):
    slots = atom_refs[0].shape[1]
    pair_count = projectors // 2
    width = projectors * LANES // 2
    atom_total = strength_ref.shape[2]
    lane = iota((LANES, LANES), 1)
    low = iota((LANES // 2, LANES), 1) < LANES // 2
    valid = (iota((projectors, atom_total), 0) < count_ref[...]).astype(F32)
    spread = (iota((projectors, width), 0) == iota((projectors, width), 1) // (LANES // 2)).astype(BF16)
    for band in range(bands):
        total = coef_refs[0][band * padded : band * padded + projectors, :]
        for away in range(1, bands):
            first = (band - away) % bands * padded
            total = total + coef_refs[away][first : first + projectors, :]
        total = total * valid
        coupled = strength_ref[:, 0, :] * total[0:1]
        for q in range(1, projectors):
            coupled = coupled + strength_ref[:, q, :] * total[q : q + 1]
        scaled = (coupled * valid).astype(BF16)
        wide_refs[band][...] = dot(scaled, spread, ((0,), (0,))).astype(BF16)
    for slab in range(CORES):

        def chunk(i, carry, slab=slab):
            at = pl.ds(pl.multiple_of(i * LANES, LANES), LANES)
            of_atom = (column(atom_refs[slab][0:1, at]) == lane).astype(BF16)
            for band in range(bands):
                total = None
                for t in range(pair_count):
                    tile = slice(t * LANES, (t + 1) * LANES)
                    term = dot(of_atom, wide_refs[band][:, tile]) * beta_refs[slab][at, tile].astype(F32)
                    total = term if total is None else total + term
                total = total + pltpu.roll(total, LANES // 2, 1)
                packed = jnp.where(low, total[: LANES // 2], total[LANES // 2 :])
                first = slab * slots // 2 + i * (LANES // 2)
                out_refs[band][pl.ds(pl.multiple_of(first, LANES // 2), LANES // 2), :] = packed.astype(BF16)
            return carry

        lax.fori_loop(0, slots // LANES, chunk, 0)


def back_project(atoms, tables, count, strength, coefs, projectors, padded):
    bands = len(coefs)
    slots = atoms[0].shape[1]
    atom_total = strength.shape[2]

    def kernel(a0, a1, b0, b1, count_ref, strength_ref, *rest):
        apply_kernel(
            bands, projectors, padded, (a0, a1), (b0, b1), count_ref, strength_ref,
            rest[:bands], rest[bands : 2 * bands], rest[2 * bands :],
        )

    return pl.pallas_call(
        kernel,
        in_specs=[VMEM_SPEC] * (6 + bands),
        out_specs=[VMEM_SPEC] * bands,
        out_shape=[jax.ShapeDtypeStruct((slots, LANES), BF16)] * bands,
        scratch_shapes=[pltpu.VMEM((atom_total, projectors * LANES // 2), BF16)] * bands,
        compiler_params=PARAMS,
    )(*atoms, *tables, count, strength, *coefs)


def place_kernel(chips, place_ref, *refs):
    block_refs, value_refs, out_ref, total = refs[: CORES * chips], refs[CORES * chips : -2], refs[-2], refs[-1]
    step = pl.program_id(0)
    slots = block_refs[0].shape[1]
    rows = out_ref.shape[1] // LANES // CORES
    low = iota((LANES // 2, LANES), 1) < LANES // 2
    for chip in range(chips):

        @pl.when(step == chip)
        def _(chip=chip):
            for slab in range(CORES):
                place = place_ref[1] if slab == 0 else CORES - 1 - place_ref[1]
                block_ref = block_refs[chip * CORES + slab]
                parts = []
                for i in range(slots // LANES):
                    odd = jnp.bitwise_and(column(block_ref[0:1, i * LANES : (i + 1) * LANES]), 1) == 1
                    first = slab * slots // 2 + i * (LANES // 2)
                    value = value_refs[chip][first : first + LANES // 2, :].astype(F32)
                    turned = pltpu.roll(value, LANES // 2, 1)
                    odd_a, odd_b = odd[: LANES // 2], odd[LANES // 2 :]
                    part_a = jnp.where(odd_a, turned, value)
                    part_b = jnp.where(odd_b, value, turned)
                    parts.append(jnp.where(low != odd_a, part_a, 0.0).astype(BF16))
                    parts.append(jnp.where(low != odd_b, part_b, 0.0).astype(BF16))
                values = jnp.concatenate(parts, axis=0)
                wanted = jnp.right_shift(block_ref[...], 1)
                for t in range(rows // LANES):
                    hits = (iota((LANES, slots), 0) + t * LANES == wanted).astype(BF16)
                    total[t * LANES : (t + 1) * LANES, :] = dot(hits, values).astype(BF16)
                start = place * rows * LANES

                def move(i, carry):
                    part = total[pl.ds(pl.multiple_of(i * 16, 16), 16), :]
                    out_ref[0:1, pl.ds(pl.multiple_of(start + i * 2048, 2048), 2048)] = part.reshape(1, 2048)
                    return carry

                lax.fori_loop(0, rows // 16, move, 0, unroll=8)


def place_rows(place, blocks, values, points):
    chips = len(values)
    share = points // chips
    whole = lambda i, place: (0, 0)
    return pl.pallas_call(
        functools.partial(place_kernel, chips),
        grid_spec=pltpu.PrefetchScalarGridSpec(
            num_scalar_prefetch=1,
            grid=(chips,),
            in_specs=[pl.BlockSpec(x.shape, whole) for x in (*blocks, *values)],
            out_specs=pl.BlockSpec((1, share), lambda i, place: (0, lax.rem(place[0] + i, chips))),
            scratch_shapes=[pltpu.VMEM((share // LANES // CORES, LANES), BF16)],
        ),
        out_shape=jax.ShapeDtypeStruct((1, points), BF16),
        compiler_params=PARAMS,
    )(place, *blocks, *values)


def body(slabs, psi, beta, pair_atom, pair_block, proj_count, strength):
    chips = slabs // CORES
    atom_total, projectors = strength.shape[:2]
    padded = -(-projectors // 8) * 8
    position = lax.axis_index("slab").astype(jnp.int32)
    chip, core = position // CORES, lax.rem(position, CORES)

    def turn(x, chips_on):
        return lax.ppermute(x, "slab", [(i, (i + CORES * chips_on) % slabs) for i in range(slabs)])

    def swap(x):
        return lax.ppermute(x, "slab", [(i, i ^ 1) for i in range(slabs)])

    rows = to_rows(psi, chip, chips)
    values = [rows[0]] + [turn(rows[away], away) for away in range(1, chips)]
    own_tables = lax.all_gather(beta[0], "band", axis=0, tiled=True)
    ids = swap(jnp.concatenate([pair_atom, pair_block], axis=0))
    atoms = (pair_atom, ids[0:1])
    blocks = (pair_block, ids[1:2])
    tables = (own_tables, swap(own_tables))
    coef = project(core, atoms, blocks, tables, values, projectors, padded, atom_total)
    coefs = [coef] + [turn(coef, away) for away in range(1, chips)]
    results = back_project(
        atoms, tables, proj_count.reshape(1, atom_total), strength.transpose(1, 2, 0), coefs, projectors, padded
    )
    results = [results[0]] + [turn(results[away], -away) for away in range(1, chips)]
    both = jnp.concatenate(blocks, axis=0)
    taken = [both] + [turn(both, -away) for away in range(1, chips)]
    block_rows = [x[s : s + 1] for x in taken for s in range(CORES)]
    return place_rows(jnp.stack([chip, core]), block_rows, results, psi.shape[1])


def solution(mesh):
    placed = (
        P(("band", "slab"), None),
        P("slab", "band", None),
        P("slab", None),
        P("slab", None),
        P(),
        P(),
    )
    return jax.shard_map(
        functools.partial(body, mesh.shape["slab"]),
        mesh=mesh,
        in_specs=placed,
        out_specs=P(("band", "slab"), None),
        check_vma=False,
    )
```

```python
import functools

import jax
import jax.numpy as jnp
from jax import lax
from jax.experimental import pallas as pl
from jax.experimental.pallas import tpu as pltpu
from jax.sharding import PartitionSpec as P

CORES = 2
LANES = 128
GROUP = 16
F32 = jnp.float32
BF16 = jnp.bfloat16
VMEM_SPEC = pl.BlockSpec(memory_space=pltpu.VMEM)
SMEM_SPEC = pl.BlockSpec(memory_space=pltpu.SMEM)
PARAMS = pltpu.CompilerParams(vmem_limit_bytes=40 * 1024 * 1024)


def dot(a, b, contract=((1,), (0,))):
    return lax.dot_general(a, b, (contract, ((), ())), preferred_element_type=F32)


def two_terms(x):
    high = x.astype(BF16)
    return high, (x - high.astype(F32)).astype(BF16)


def iota(shape, axis):
    return lax.broadcasted_iota(jnp.int32, shape, axis)


def ids_row(ref, place_ref, piece, share):
    if share == ref.shape[1]:
        return ref[...]
    first = jnp.bitwise_xor(place_ref[1], piece) * share
    return ref[0:1, pl.ds(pl.multiple_of(first, share), share)]


def ids_column(ref, place_ref, piece, share):
    row = ids_row(ref, place_ref, piece, share)
    parts = [
        jnp.transpose(jnp.broadcast_to(row[:, i * LANES : (i + 1) * LANES], (LANES, LANES)))
        for i in range(share // LANES)
    ]
    return jnp.concatenate(parts, axis=0)


def rows_kernel(place_ref, psi_ref, *out_refs):
    step = pl.program_id(0)
    for index, out_ref in enumerate(out_refs):

        @pl.when(step == index)
        def _(out_ref=out_ref):
            def move(i, carry):
                part = psi_ref[0:1, pl.ds(pl.multiple_of(i * 2048, 2048), 2048)]
                out_ref[pl.ds(pl.multiple_of(i * 16, 16), 16), :] = part.reshape(16, LANES)
                return carry

            lax.fori_loop(0, out_ref.shape[0] // 16, move, 0, unroll=8)


def to_rows(psi, chip, chips):
    points = psi.shape[1] // chips
    rows = points // LANES
    return pl.pallas_call(
        rows_kernel,
        grid_spec=pltpu.PrefetchScalarGridSpec(
            num_scalar_prefetch=1,
            grid=(chips,),
            in_specs=[pl.BlockSpec((1, points), lambda i, chip: (0, lax.rem(chip[0] + i, chips)))],
            out_specs=[pl.BlockSpec((rows, LANES), lambda i, chip: (0, 0))] * chips,
        ),
        out_shape=[jax.ShapeDtypeStruct((rows, LANES), BF16)] * chips,
        compiler_params=PARAMS,
    )(chip.reshape(1), psi)


def project_kernel(bands, projectors, padded, pieces, place_ref, atom_refs, block_refs, beta_refs, psi_refs, coef_ref, picks, highs, rests):
    slots = atom_refs[0].shape[1]
    share = slots // pieces
    slab_rows = psi_refs[0].shape[0] // CORES
    pair_count = projectors // 2
    wide = 2 * bands * GROUP
    lane = iota((share, LANES), 1)
    low = lane < LANES // 2
    source = iota((pair_count * wide, bands * padded), 0) // GROUP
    target = iota((pair_count * wide, bands * padded), 1)
    gather_lanes = (target == lax.rem(source, bands) * padded + source // bands).astype(BF16)
    diagonal = lax.rem(iota((GROUP, wide), 0), GROUP) == lax.rem(iota((GROUP, wide), 1), GROUP)
    for slab in range(CORES):
        place = place_ref[0] if slab == 0 else CORES - 1 - place_ref[0]
        first_row = pl.multiple_of(place * slab_rows, slab_rows)
        hits, odds, of_atom = [], [], []
        for piece in range(pieces):
            blocks = ids_column(block_refs[slab], place_ref, piece, share)
            wanted = jnp.right_shift(blocks, 1)
            odds.append(jnp.bitwise_and(blocks, 1) == 1)
            hits.append(
                jnp.concatenate([(wanted - t * LANES == lane).astype(BF16) for t in range(slab_rows // LANES)], axis=1)
            )
            of_atom.append((ids_column(atom_refs[slab], place_ref, piece, share) == lane).astype(BF16))
        hits = jnp.concatenate(hits, axis=0)
        for band, psi_ref in enumerate(psi_refs):
            picked = dot(hits, psi_ref[pl.ds(first_row, slab_rows), :])
            for piece in range(pieces):
                rows = slice(piece * share, (piece + 1) * share)
                straight = picked[rows]
                turned = pltpu.roll(straight, LANES // 2, 1)
                both = jnp.where(low == odds[piece], turned, straight)
                picks[band, rows, :] = jnp.where(low, both, 0.0).astype(BF16)
                picks[bands + band, rows, :] = jnp.where(low, 0.0, both).astype(BF16)
        for piece in range(pieces):
            table_ref = beta_refs[slab * pieces + piece]
            for group in range(share // GROUP):
                own = slice(group * GROUP, (group + 1) * GROUP)
                rows = slice(piece * share + group * GROUP, piece * share + (group + 1) * GROUP)
                values = jnp.concatenate([picks[part, rows, :] for part in range(2 * bands)], axis=0)
                tables = jnp.concatenate([table_ref[own, t * LANES : (t + 1) * LANES] for t in range(pair_count)], axis=0)
                crossed = dot(tables, values, ((1,), (1,)))
                for t in range(pair_count):
                    kept = jnp.where(diagonal, crossed[t * GROUP : (t + 1) * GROUP], 0.0)
                    highs[rows, t * wide : (t + 1) * wide], rests[rows, t * wide : (t + 1) * wide] = two_terms(kept)
        slot_coef = dot(highs[...], gather_lanes) + dot(rests[...], gather_lanes)
        high, rest = two_terms(slot_coef)
        of_atom = jnp.concatenate(of_atom, axis=0)
        summed = dot(high, of_atom, ((0,), (0,))) + dot(rest, of_atom, ((0,), (0,)))
        if slab == 0:
            coef_ref[...] = summed
        else:
            coef_ref[...] += summed


def project(place, atoms, blocks, tables, values, projectors, padded, atom_total):
    bands = len(values)
    pieces = len(tables) // CORES
    slots = atoms[0].shape[1]
    width = projectors * bands * GROUP

    def kernel(place_ref, a0, a1, k0, k1, *rest):
        refs = [rest[: len(tables)], rest[len(tables) : len(tables) + bands], rest[len(tables) + bands :]]
        project_kernel(bands, projectors, padded, pieces, place_ref, (a0, a1), (k0, k1), refs[0], refs[1], *refs[2])

    return pl.pallas_call(
        kernel,
        in_specs=[SMEM_SPEC] + [VMEM_SPEC] * (4 + len(tables) + bands),
        out_specs=VMEM_SPEC,
        out_shape=jax.ShapeDtypeStruct((bands * padded, atom_total), F32),
        scratch_shapes=[pltpu.VMEM((2 * bands, slots, LANES), BF16)] + [pltpu.VMEM((slots, width), BF16)] * 2,
        compiler_params=PARAMS,
    )(place, *atoms, *blocks, *tables, *values)


def apply_kernel(bands, projectors, padded, pieces, place_ref, atom_refs, beta_refs, count_ref, strength_ref, coef_refs, out_refs, wide_refs):
    slots = atom_refs[0].shape[1]
    share = slots // pieces
    pair_count = projectors // 2
    width = projectors * LANES // 2
    atom_total = strength_ref.shape[2]
    lane = iota((share, LANES), 1)
    low = iota((LANES // 2, LANES), 1) < LANES // 2
    valid = (iota((projectors, atom_total), 0) < count_ref[...]).astype(F32)
    spread = (iota((projectors, width), 0) == iota((projectors, width), 1) // (LANES // 2)).astype(BF16)
    for band in range(bands):
        total = coef_refs[0][band * padded : band * padded + projectors, :]
        for away in range(1, bands):
            first = (band - away) % bands * padded
            total = total + coef_refs[away][first : first + projectors, :]
        total = total * valid
        coupled = strength_ref[:, 0, :] * total[0:1]
        for q in range(1, projectors):
            coupled = coupled + strength_ref[:, q, :] * total[q : q + 1]
        scaled = (coupled * valid).astype(BF16)
        wide_refs[band][...] = dot(scaled, spread, ((0,), (0,))).astype(BF16)
    for slab in range(CORES):
        of_atom = [
            (ids_column(atom_refs[slab], place_ref, piece, share) == lane).astype(BF16) for piece in range(pieces)
        ]
        for band in range(bands):
            for piece in range(pieces):
                total = None
                for t in range(pair_count):
                    tile = slice(t * LANES, (t + 1) * LANES)
                    term = dot(of_atom[piece], wide_refs[band][:, tile]) * beta_refs[slab * pieces + piece][:, tile].astype(F32)
                    total = term if total is None else total + term
                total = total + pltpu.roll(total, LANES // 2, 1)
                for i in range(share // LANES):
                    part = total[i * LANES : (i + 1) * LANES]
                    packed = jnp.where(low, part[: LANES // 2], part[LANES // 2 :])
                    first = (slab * slots + piece * share + i * LANES) // 2
                    out_refs[band][first : first + LANES // 2, :] = packed.astype(BF16)


def back_project(place, atoms, tables, count, strength, coefs, projectors, padded):
    bands = len(coefs)
    pieces = len(tables) // CORES
    slots = atoms[0].shape[1]
    atom_total = strength.shape[2]

    def kernel(place_ref, a0, a1, count_ref, strength_ref, *rest):
        ends = [len(tables), len(tables) + bands, len(tables) + 2 * bands]
        apply_kernel(
            bands, projectors, padded, pieces, place_ref, (a0, a1), rest[: ends[0]], count_ref, strength_ref,
            rest[ends[0] : ends[1]], rest[ends[1] : ends[2]], rest[ends[2] :],
        )

    return pl.pallas_call(
        kernel,
        in_specs=[SMEM_SPEC] + [VMEM_SPEC] * (4 + len(tables) + bands),
        out_specs=[VMEM_SPEC] * bands,
        out_shape=[jax.ShapeDtypeStruct((slots, LANES), BF16)] * bands,
        scratch_shapes=[pltpu.VMEM((atom_total, projectors * LANES // 2), BF16)] * bands,
        compiler_params=PARAMS,
    )(place, *atoms, count, strength, *tables, *coefs)


def place_kernel(chips, pieces, place_ref, *refs):
    block_refs, value_refs, out_ref = refs[: CORES * chips], refs[CORES * chips : -1], refs[-1]
    step = pl.program_id(0)
    slots = block_refs[0].shape[1]
    share = slots // pieces
    rows = out_ref.shape[1] // LANES // CORES
    low = iota((LANES // 2, LANES), 1) < LANES // 2
    for chip in range(chips):

        @pl.when(step == chip)
        def _(chip=chip):
            for slab in range(CORES):
                place = place_ref[0] if slab == 0 else CORES - 1 - place_ref[0]
                block_ref = block_refs[chip * CORES + slab]
                parts, wanted = [], []
                for piece in range(pieces):
                    blocks = ids_column(block_ref, place_ref, piece, share)
                    wanted.append(jnp.right_shift(ids_row(block_ref, place_ref, piece, share), 1))
                    for i in range(share // LANES):
                        odd = jnp.bitwise_and(blocks[i * LANES : (i + 1) * LANES], 1) == 1
                        first = (slab * slots + piece * share + i * LANES) // 2
                        value = value_refs[chip][first : first + LANES // 2, :].astype(F32)
                        turned = pltpu.roll(value, LANES // 2, 1)
                        odd_a, odd_b = odd[: LANES // 2], odd[LANES // 2 :]
                        part_a = jnp.where(odd_a, turned, value)
                        part_b = jnp.where(odd_b, value, turned)
                        parts.append(jnp.where(low != odd_a, part_a, 0.0).astype(BF16))
                        parts.append(jnp.where(low != odd_b, part_b, 0.0).astype(BF16))
                values = jnp.concatenate(parts, axis=0)
                wanted = jnp.concatenate(wanted, axis=1)
                start = place * rows * LANES
                for t in range(rows // LANES):
                    hits = (iota((LANES, slots), 0) + t * LANES == wanted).astype(BF16)
                    total = dot(hits, values).astype(BF16)
                    for i in range(LANES // 16):
                        at = pl.multiple_of(start + t * LANES * LANES + i * 2048, 2048)
                        out_ref[0:1, pl.ds(at, 2048)] = total[i * 16 : (i + 1) * 16].reshape(1, 2048)


def place_rows(place, blocks, values, points, pieces):
    chips = len(values)
    share = points // chips
    whole = lambda i, place: (0, 0)
    return pl.pallas_call(
        functools.partial(place_kernel, chips, pieces),
        grid_spec=pltpu.PrefetchScalarGridSpec(
            num_scalar_prefetch=1,
            grid=(chips,),
            in_specs=[pl.BlockSpec(x.shape, whole) for x in (*blocks, *values)],
            out_specs=pl.BlockSpec((1, share), lambda i, place: (0, lax.rem(place[2] + i, chips))),
        ),
        out_shape=jax.ShapeDtypeStruct((1, points), BF16),
        compiler_params=PARAMS,
    )(place, *blocks, *values)


def body(bands, slabs, psi, beta, pair_atom, pair_block, proj_count, strength):
    chips = slabs // CORES
    atom_total, projectors = strength.shape[:2]
    padded = -(-projectors // 8) * 8
    position = lax.axis_index("slab").astype(jnp.int32)
    chip, core = position // CORES, lax.rem(position, CORES)
    place = jnp.stack([core, lax.axis_index("band").astype(jnp.int32), chip])

    def turn(x, chips_on):
        return lax.ppermute(x, "slab", [(i, (i + CORES * chips_on) % slabs) for i in range(slabs)])

    def swap(x):
        return lax.ppermute(x, "slab", [(i, i ^ 1) for i in range(slabs)])

    def across(x, bit):
        return lax.ppermute(x, "band", [(i, i ^ bit) for i in range(bands)])

    if beta.shape[1] % LANES == 0 and bands & (bands - 1) == 0:
        tables = [beta[0]] + [across(beta[0], bit) for bit in range(1, bands)]
    else:
        tables = [lax.all_gather(beta[0], "band", axis=0, tiled=True)]
    tables = tables + [swap(x) for x in tables]
    rows = to_rows(psi, chip, chips)
    values = [rows[0]] + [turn(rows[away], away) for away in range(1, chips)]
    ids = swap(jnp.concatenate([pair_atom, pair_block], axis=0))
    atoms = (pair_atom, ids[0:1])
    blocks = (pair_block, ids[1:2])
    coef = project(place, atoms, blocks, tables, values, projectors, padded, atom_total)
    coefs = [coef] + [turn(coef, away) for away in range(1, chips)]
    results = back_project(
        place, atoms, tables, proj_count.reshape(1, atom_total), strength.transpose(1, 2, 0), coefs, projectors, padded
    )
    results = [results[0]] + [turn(results[away], -away) for away in range(1, chips)]
    both = jnp.concatenate(blocks, axis=0)
    taken = [both] + [turn(both, -away) for away in range(1, chips)]
    block_rows = [x[s : s + 1] for x in taken for s in range(CORES)]
    return place_rows(place, block_rows, results, psi.shape[1], len(tables) // CORES)


def solution(mesh):
    placed = (
        P(("band", "slab"), None),
        P("slab", "band", None),
        P("slab", None),
        P("slab", None),
        P(),
        P(),
    )
    return jax.shard_map(
        functools.partial(body, mesh.shape["band"], mesh.shape["slab"]),
        mesh=mesh,
        in_specs=placed,
        out_specs=P(("band", "slab"), None),
        check_vma=False,
    )
```

```python
import functools

import jax
import jax.numpy as jnp
from jax import lax
from jax.experimental import pallas as pl
from jax.experimental.pallas import tpu as pltpu
from jax.sharding import PartitionSpec as P

CORES = 2
LANES = 128
GROUP = 16
GATHER_BYTES = 10_000_000
F32 = jnp.float32
BF16 = jnp.bfloat16
VMEM_SPEC = pl.BlockSpec(memory_space=pltpu.VMEM)
SMEM_SPEC = pl.BlockSpec(memory_space=pltpu.SMEM)
PARAMS = pltpu.CompilerParams(vmem_limit_bytes=40 * 1024 * 1024)


def dot(a, b, contract=((1,), (0,))):
    return lax.dot_general(a, b, (contract, ((), ())), preferred_element_type=F32)


def two_terms(x):
    high = x.astype(BF16)
    return high, (x - high.astype(F32)).astype(BF16)


def after(x, *others):
    return lax.optimization_barrier((x, *others))[0]


def iota(shape, axis):
    return lax.broadcasted_iota(jnp.int32, shape, axis)


def slab_index(place_ref, chips, away, slab):
    core = place_ref[0] if slab == 0 else CORES - 1 - place_ref[0]
    return lax.rem(place_ref[2] + away, chips) * CORES + core


def slot_ids(ids_ref, place_ref, index, pieces, kind):
    slot_rows = ids_ref.shape[1] // 2
    share = slot_rows // pieces
    for piece in range(pieces):
        first = 0 if pieces == 1 else jnp.bitwise_xor(place_ref[1], piece) * share
        for i in range(share):
            yield ids_ref[index, pl.ds(kind * slot_rows + first + i, 1), :]


def down(ids):
    return jnp.transpose(jnp.broadcast_to(ids, (LANES, LANES)))


def rows_kernel(psi_ref, out_ref):
    def move(i, carry):
        part = psi_ref[0:1, pl.ds(pl.multiple_of(i * 2048, 2048), 2048)]
        out_ref[pl.ds(pl.multiple_of(i * 16, 16), 16), :] = part.reshape(16, LANES)
        return carry

    lax.fori_loop(0, out_ref.shape[0] // 16, move, 0, unroll=8)


def to_rows(psi):
    rows = psi.shape[1] // LANES
    return pl.pallas_call(
        rows_kernel,
        in_specs=[VMEM_SPEC],
        out_specs=VMEM_SPEC,
        out_shape=jax.ShapeDtypeStruct((rows, LANES), BF16),
        compiler_params=PARAMS,
    )(psi)


def gather_kernel(pieces, place_ref, ids_ref, rows_ref, out_refs):
    slots = ids_ref.shape[1] // 2 * LANES
    chips = len(out_refs)
    slab_rows = rows_ref.shape[0] // (CORES * chips)
    lane = iota((LANES, LANES), 1)
    low = iota((LANES // 2, LANES), 1) < LANES // 2
    for away, out_ref in enumerate(out_refs):
        for slab in range(CORES):
            index = slab_index(place_ref, chips, away, slab)
            odds, hits = [], []
            for ids in slot_ids(ids_ref, place_ref, index, pieces, 0):
                blocks = down(ids)
                wanted = jnp.right_shift(blocks, 1)
                odds.append(jnp.bitwise_and(blocks, 1) == 1)
                hits.append(
                    jnp.concatenate([(wanted - t * LANES == lane).astype(BF16) for t in range(slab_rows // LANES)], axis=1)
                )
            first_row = pl.multiple_of(index * slab_rows, slab_rows)
            picked = dot(jnp.concatenate(hits, axis=0), rows_ref[pl.ds(first_row, slab_rows), :])
            for i, odd in enumerate(odds):
                straight = picked[i * LANES : (i + 1) * LANES]
                turned = pltpu.roll(straight, LANES // 2, 1)
                lower = jnp.where(odd, turned, straight)[: LANES // 2]
                upper = jnp.where(odd, straight, turned)[LANES // 2 :]
                first = (slab * slots + i * LANES) // 2
                out_ref[first : first + LANES // 2, :] = jnp.where(low, lower, upper).astype(BF16)


def gather(place, ids, rows, pieces, chips):
    slots = ids.shape[1] // 2 * LANES

    def kernel(place_ref, ids_ref, rows_ref, *out_refs):
        gather_kernel(pieces, place_ref, ids_ref, rows_ref, out_refs)

    return pl.pallas_call(
        kernel,
        in_specs=[SMEM_SPEC] + [VMEM_SPEC] * 2,
        out_specs=[VMEM_SPEC] * chips,
        out_shape=[jax.ShapeDtypeStruct((slots, LANES), BF16)] * chips,
        cost_estimate=pl.CostEstimate(flops=0, bytes_accessed=GATHER_BYTES, transcendentals=0),
        compiler_params=PARAMS,
    )(place, ids, rows)


def project_kernel(projectors, padded, pieces, place_ref, ids_ref, table_refs, packed_refs, coef_ref, picks_of, highs, rests):
    bands = len(packed_refs)
    slots = table_refs[0].shape[0]
    pair_count = projectors // 2
    wide = 2 * bands * GROUP
    lane = iota((LANES, LANES), 1)
    low = iota((bands * GROUP, LANES), 1) < LANES // 2
    source = iota((pair_count * wide, bands * padded), 0) // GROUP
    target = iota((pair_count * wide, bands * padded), 1)
    gather_lanes = (target == lax.rem(source, bands) * padded + source // bands).astype(BF16)
    diagonal = lax.rem(iota((GROUP, wide), 0), GROUP) == lax.rem(iota((GROUP, wide), 1), GROUP)
    none = jnp.zeros((bands * GROUP, LANES), BF16)
    half = LANES // 2
    left = iota((half, LANES), 1) < half
    for band, packed_ref in enumerate(packed_refs):
        for i in range(CORES * slots // LANES):
            straight = packed_ref[i * half : (i + 1) * half, :].astype(F32)
            turned = pltpu.roll(straight, half, 1)
            picks_of[band, i * LANES : i * LANES + half, :] = jnp.where(left, straight, turned).astype(BF16)
            picks_of[band, i * LANES + half : (i + 1) * LANES, :] = jnp.where(left, turned, straight).astype(BF16)
    for slab, table_ref in enumerate(table_refs):
        index = slab_index(place_ref, ids_ref.shape[0] // CORES, 0, slab)
        atoms = slot_ids(ids_ref, place_ref, index, pieces, 1)
        of_atom = jnp.concatenate([(down(ids) == lane).astype(BF16) for ids in atoms], axis=0)
        for group in range(slots // GROUP):
            rows = slice(group * GROUP, (group + 1) * GROUP)
            picked = slice(slab * slots + group * GROUP, slab * slots + (group + 1) * GROUP)
            picks = jnp.concatenate([picks_of[band, picked, :] for band in range(bands)], axis=0)
            values = jnp.concatenate([jnp.where(low, picks, none), jnp.where(low, none, picks)], axis=0)
            tables = jnp.concatenate([table_ref[rows, t * LANES : (t + 1) * LANES] for t in range(pair_count)], axis=0)
            crossed = dot(tables, values, ((1,), (1,)))
            for t in range(pair_count):
                kept = jnp.where(diagonal, crossed[t * GROUP : (t + 1) * GROUP], 0.0)
                highs[rows, t * wide : (t + 1) * wide], rests[rows, t * wide : (t + 1) * wide] = two_terms(kept)
        slot_coef = dot(highs[...], gather_lanes) + dot(rests[...], gather_lanes)
        high, rest = two_terms(slot_coef)
        summed = dot(high, of_atom, ((0,), (0,))) + dot(rest, of_atom, ((0,), (0,)))
        coef_ref[...] = summed if slab == 0 else coef_ref[...] + summed


def project(place, ids, tables, picks, projectors, padded, pieces):
    bands = len(picks)
    slots = tables[0].shape[0]
    width = projectors * bands * GROUP

    def kernel(place_ref, ids_ref, own_ref, other_ref, *rest):
        project_kernel(projectors, padded, pieces, place_ref, ids_ref, (own_ref, other_ref), rest[:bands], *rest[bands:])

    return pl.pallas_call(
        kernel,
        in_specs=[SMEM_SPEC] + [VMEM_SPEC] * (3 + bands),
        out_specs=VMEM_SPEC,
        out_shape=jax.ShapeDtypeStruct((bands * padded, LANES), F32),
        scratch_shapes=[pltpu.VMEM((bands, CORES * slots, LANES), BF16)] + [pltpu.VMEM((slots, width), BF16)] * 2,
        compiler_params=PARAMS,
    )(place, ids, *tables, *picks)


def apply_kernel(bands, projectors, padded, pieces, place_ref, ids_ref, table_refs, count_ref, strength_ref, coef_refs, out_refs, wide_refs):
    slots = table_refs[0].shape[0]
    pair_count = projectors // 2
    width = projectors * LANES // 2
    atom_total = strength_ref.shape[2]
    lane = iota((LANES, LANES), 1)
    low = iota((LANES // 2, LANES), 1) < LANES // 2
    valid = (iota((projectors, atom_total), 0) < count_ref[...]).astype(F32)
    spread = (iota((projectors, width), 0) == iota((projectors, width), 1) // (LANES // 2)).astype(BF16)
    for band in range(bands):
        total = coef_refs[0][band * padded : band * padded + projectors, :]
        for away in range(1, bands):
            first = (band - away) % bands * padded
            total = total + coef_refs[away][first : first + projectors, :]
        total = total * valid
        coupled = strength_ref[:, 0, :] * total[0:1]
        for q in range(1, projectors):
            coupled = coupled + strength_ref[:, q, :] * total[q : q + 1]
        scaled = (coupled * valid).astype(BF16)
        wide_refs[band][...] = dot(scaled, spread, ((0,), (0,))).astype(BF16)
    for slab, table_ref in enumerate(table_refs):
        index = slab_index(place_ref, ids_ref.shape[0] // CORES, 0, slab)
        for i, atoms in enumerate(slot_ids(ids_ref, place_ref, index, pieces, 1)):
            of_atom = (down(atoms) == lane).astype(BF16)
            rows = slice(i * LANES, (i + 1) * LANES)
            first = (slab * slots + i * LANES) // 2
            for band in range(bands):
                total = None
                for t in range(pair_count):
                    tile = slice(t * LANES, (t + 1) * LANES)
                    term = dot(of_atom, wide_refs[band][:, tile]) * table_ref[rows, tile].astype(F32)
                    total = term if total is None else total + term
                total = total + pltpu.roll(total, LANES // 2, 1)
                packed = jnp.where(low, total[: LANES // 2], total[LANES // 2 :])
                out_refs[band][first : first + LANES // 2, :] = packed.astype(BF16)


def back_project(place, ids, tables, count, strength, coefs, projectors, padded, pieces):
    bands = len(coefs)
    slots = tables[0].shape[0]
    atom_total = strength.shape[2]

    def kernel(place_ref, ids_ref, own_ref, other_ref, count_ref, strength_ref, *rest):
        apply_kernel(
            bands, projectors, padded, pieces, place_ref, ids_ref, (own_ref, other_ref), count_ref, strength_ref,
            rest[:bands], rest[bands : 2 * bands], rest[2 * bands :],
        )

    return pl.pallas_call(
        kernel,
        in_specs=[SMEM_SPEC] + [VMEM_SPEC] * (5 + bands),
        out_specs=[VMEM_SPEC] * bands,
        out_shape=[jax.ShapeDtypeStruct((slots, LANES), BF16)] * bands,
        scratch_shapes=[pltpu.VMEM((atom_total, projectors * LANES // 2), BF16)] * bands,
        compiler_params=PARAMS,
    )(place, ids, *tables, count, strength, *coefs)


def place_kernel(chips, pieces, place_ref, *refs):
    ids_ref, value_refs, out_ref = refs[0], refs[1:-1], refs[-1]
    step = pl.program_id(0)
    slots = ids_ref.shape[1] // 2 * LANES
    rows = out_ref.shape[1] // LANES // CORES
    low = iota((LANES // 2, LANES), 1) < LANES // 2
    for chip in range(chips):

        @pl.when(step == chip)
        def _(chip=chip):
            for slab in range(CORES):
                place = place_ref[0] if slab == 0 else CORES - 1 - place_ref[0]
                index = slab_index(place_ref, chips, chip, slab)
                parts, wanted = [], []
                for i, blocks in enumerate(slot_ids(ids_ref, place_ref, index, pieces, 0)):
                    wanted.append(jnp.right_shift(blocks, 1))
                    odd = jnp.bitwise_and(down(blocks), 1) == 1
                    first = (slab * slots + i * LANES) // 2
                    value = value_refs[chip][first : first + LANES // 2, :].astype(F32)
                    turned = pltpu.roll(value, LANES // 2, 1)
                    odd_a, odd_b = odd[: LANES // 2], odd[LANES // 2 :]
                    part_a = jnp.where(odd_a, turned, value)
                    part_b = jnp.where(odd_b, value, turned)
                    parts.append(jnp.where(low != odd_a, part_a, 0.0).astype(BF16))
                    parts.append(jnp.where(low != odd_b, part_b, 0.0).astype(BF16))
                values = jnp.concatenate(parts, axis=0)
                wanted = jnp.concatenate(wanted, axis=1)
                start = place * rows * LANES
                for t in range(rows // LANES):
                    hits = (iota((LANES, slots), 0) + t * LANES == wanted).astype(BF16)
                    total = dot(hits, values).astype(BF16)
                    for i in range(LANES // 16):
                        at = pl.multiple_of(start + t * LANES * LANES + i * 2048, 2048)
                        out_ref[0:1, pl.ds(at, 2048)] = total[i * 16 : (i + 1) * 16].reshape(1, 2048)


def place_rows(place, ids, values, points, pieces):
    chips = len(values)
    share = points // chips
    return pl.pallas_call(
        functools.partial(place_kernel, chips, pieces),
        grid_spec=pltpu.PrefetchScalarGridSpec(
            num_scalar_prefetch=1,
            grid=(chips,),
            in_specs=[pl.BlockSpec(x.shape, lambda i, place, rank=x.ndim: (0,) * rank) for x in (ids, *values)],
            out_specs=pl.BlockSpec((1, share), lambda i, place: (0, lax.rem(place[2] + i, chips))),
        ),
        out_shape=jax.ShapeDtypeStruct((1, points), BF16),
        compiler_params=PARAMS,
    )(place, ids, *values)


def body(bands, slabs, psi, beta, pair_atom, pair_block, proj_count, strength):
    chips = slabs // CORES
    atom_total, projectors = strength.shape[:2]
    padded = -(-projectors // 8) * 8
    position = lax.axis_index("slab").astype(jnp.int32)
    chip, core = position // CORES, lax.rem(position, CORES)
    place = jnp.stack([core, lax.axis_index("band").astype(jnp.int32), chip])

    def turn(x, chips_on):
        return lax.ppermute(x, "slab", [(i, (i + CORES * chips_on) % slabs) for i in range(slabs)])

    def swap(x):
        return lax.ppermute(x, "slab", [(i, i ^ 1) for i in range(slabs)])

    def across(x, bit):
        return lax.ppermute(x, "band", [(i, i ^ bit) for i in range(bands)])

    ids = jnp.concatenate([pair_block, pair_atom], axis=0).reshape(1, -1, LANES)
    ids = lax.all_to_all(jnp.broadcast_to(ids, (slabs, *ids.shape[1:])), "slab", 0, 0, tiled=True)
    rows = to_rows(psi)
    pieces = bands if beta.shape[1] % LANES == 0 and bands & (bands - 1) == 0 else 1
    if pieces > 1:
        tables = [beta[0]] + [across(beta[0], bit) for bit in range(1, bands)]
    else:
        tables = [lax.all_gather(beta[0], "band", axis=0, tiled=True)]
    picks = gather(place, ids, rows, pieces, chips)
    tables = jnp.concatenate([after(table, picks[0]) for table in tables], axis=0)
    tables = (tables, swap(tables))
    picks = [picks[0]] + [turn(picks[away], away) for away in range(1, chips)]
    coef = project(place, ids, tables, picks, projectors, padded, pieces)
    coefs = [coef] + [turn(coef, away) for away in range(1, chips)]
    count, strength = proj_count.reshape(1, atom_total), strength.transpose(1, 2, 0)
    results = back_project(place, ids, tables, count, strength, coefs, projectors, padded, pieces)
    results = [results[0]] + [turn(results[away], -away) for away in range(1, chips)]
    return place_rows(place, ids, results, psi.shape[1], pieces)


def solution(mesh):
    placed = (
        P(("band", "slab"), None),
        P("slab", "band", None),
        P("slab", None),
        P("slab", None),
        P(),
        P(),
    )
    return jax.shard_map(
        functools.partial(body, mesh.shape["band"], mesh.shape["slab"]),
        mesh=mesh,
        in_specs=placed,
        out_specs=P(("band", "slab"), None),
        check_vma=False,
    )
```

```python
import functools

import jax
import jax.numpy as jnp
from jax import lax
from jax.experimental import pallas as pl
from jax.experimental.pallas import tpu as pltpu
from jax.sharding import PartitionSpec as P

CORES = 2
LANES = 128
CHIPS = 4
PARTNERS = 4
PIECES = 4
GROUP = 16
HALVES = 2
GATHER_BYTES = 10_000_000
PROJECT_BYTES = 30_000_000
F32 = jnp.float32
BF16 = jnp.bfloat16
VMEM_SPEC = pl.BlockSpec(memory_space=pltpu.VMEM)
SMEM_SPEC = pl.BlockSpec(memory_space=pltpu.SMEM)
PARAMS = pltpu.CompilerParams(vmem_limit_bytes=40 * 1024 * 1024)


def dot(a, b, contract=((1,), (0,))):
    return lax.dot_general(a, b, (contract, ((), ())), preferred_element_type=F32)


def two_terms(x):
    high = x.astype(BF16)
    return high, (x - high.astype(F32)).astype(BF16)


def after(x, *others):
    return lax.optimization_barrier((x, *others))[0]


def iota(shape, axis):
    return lax.broadcasted_iota(jnp.int32, shape, axis)


def slab_index(place_ref, turned, slab):
    core = place_ref[0] if slab == 0 else CORES - 1 - place_ref[0]
    return jnp.bitwise_xor(place_ref[2], turned) * CORES + core


def owner(turned_chip, turned_column):
    return (turned_chip & 1) | (turned_column & 2), (turned_chip & 2) | (turned_column & 1)


def pieces_of(half_index):
    return range(half_index * PIECES // HALVES, (half_index + 1) * PIECES // HALVES)


def slot_ids(ids_ref, place_ref, slab, turned_chip, turned_column, kind):
    slot_rows = ids_ref.shape[1] // 2
    share = slot_rows // PARTNERS
    index = slab_index(place_ref, turned_chip, slab)
    first = kind * slot_rows + jnp.bitwise_xor(place_ref[1], turned_column) * share
    return [ids_ref[index, pl.ds(first + i, 1), :] for i in range(share)]


def atom_hits(ids_ref, place_ref, slab, pieces):
    lane = iota((LANES, LANES), 1)
    for piece in pieces:
        for atoms in slot_ids(ids_ref, place_ref, slab, piece & 2, piece & 1, 1):
            yield (down(atoms) == lane).astype(BF16)


def down(ids):
    return jnp.transpose(jnp.broadcast_to(ids, (LANES, LANES)))


def rows_kernel(psi_ref, out_ref):
    def move(i, carry):
        part = psi_ref[0:1, pl.ds(pl.multiple_of(i * 2048, 2048), 2048)]
        out_ref[pl.ds(pl.multiple_of(i * 16, 16), 16), :] = part.reshape(16, LANES)
        return carry

    lax.fori_loop(0, out_ref.shape[0] // 16, move, 0, unroll=8)


def to_rows(psi):
    rows = psi.shape[1] // LANES
    return pl.pallas_call(
        rows_kernel,
        in_specs=[VMEM_SPEC],
        out_specs=VMEM_SPEC,
        out_shape=jax.ShapeDtypeStruct((rows, LANES), BF16),
        compiler_params=PARAMS,
    )(psi)


def gather_kernel(place_ref, ids_ref, rows_ref, out_refs):
    half = LANES // 2
    slab_rows = rows_ref.shape[0] // (CORES * CHIPS)
    lane = iota((LANES, LANES), 1)
    low = iota((half, LANES), 1) < half
    for chip in range(CHIPS):
        for slab in range(CORES):
            index = slab_index(place_ref, chip, slab)
            odds, hits, places = [], [], []
            for column in range(PARTNERS):
                partner, piece = owner(chip, column)
                ids = slot_ids(ids_ref, place_ref, slab, chip, column, 0)
                for i, row in enumerate(ids):
                    blocks = down(row)
                    wanted = jnp.right_shift(blocks, 1)
                    odds.append(jnp.bitwise_and(blocks, 1) == 1)
                    hits.append(
                        jnp.concatenate([(wanted - t * LANES == lane).astype(BF16) for t in range(slab_rows // LANES)], axis=1)
                    )
                    places.append((out_refs[partner], ((slab * PIECES + piece) * len(ids) + i) * half))
            first_row = pl.multiple_of(index * slab_rows, slab_rows)
            picked = dot(jnp.concatenate(hits, axis=0), rows_ref[pl.ds(first_row, slab_rows), :])
            for i, (odd, (out_ref, first)) in enumerate(zip(odds, places)):
                straight = picked[i * LANES : (i + 1) * LANES]
                turned = pltpu.roll(straight, half, 1)
                lower = jnp.where(odd, turned, straight)[:half]
                upper = jnp.where(odd, straight, turned)[half:]
                out_ref[first : first + half, :] = jnp.where(low, lower, upper).astype(BF16)


def gather(place, ids, rows):
    slots = CORES * PIECES * ids.shape[1] // 2 * LANES // PARTNERS

    def kernel(place_ref, ids_ref, rows_ref, *out_refs):
        gather_kernel(place_ref, ids_ref, rows_ref, out_refs)

    return pl.pallas_call(
        kernel,
        in_specs=[SMEM_SPEC] + [VMEM_SPEC] * 2,
        out_specs=[VMEM_SPEC] * PARTNERS,
        out_shape=[jax.ShapeDtypeStruct((slots // 2, LANES), BF16)] * PARTNERS,
        cost_estimate=pl.CostEstimate(flops=0, bytes_accessed=GATHER_BYTES, transcendentals=0),
        compiler_params=PARAMS,
    )(place, ids, rows)


def project_kernel(projectors, padded, half_index, place_ref, ids_ref, table_refs, packed_refs, before_refs, coef_ref, picks_of, highs, rests):
    bands = len(packed_refs)
    slots = table_refs[0].shape[0]
    pair_count = projectors // 2
    wide = 2 * bands * GROUP
    low = iota((bands * GROUP, LANES), 1) < LANES // 2
    source = iota((pair_count * wide, bands * padded), 0) // GROUP
    target = iota((pair_count * wide, bands * padded), 1)
    gather_lanes = (target == lax.rem(source, bands) * padded + source // bands).astype(BF16)
    diagonal = lax.rem(iota((GROUP, wide), 0), GROUP) == lax.rem(iota((GROUP, wide), 1), GROUP)
    none = jnp.zeros((bands * GROUP, LANES), BF16)
    half = LANES // 2
    left = iota((half, LANES), 1) < half
    for band, packed_ref in enumerate(packed_refs):
        for i in range(CORES * slots // LANES):
            slab, block = divmod(i, slots // LANES)
            first = ((slab * HALVES + half_index) * (slots // LANES) + block) * half
            straight = packed_ref[first : first + half, :].astype(F32)
            turned = pltpu.roll(straight, half, 1)
            picks_of[band, i * LANES : i * LANES + half, :] = jnp.where(left, straight, turned).astype(BF16)
            picks_of[band, i * LANES + half : (i + 1) * LANES, :] = jnp.where(left, turned, straight).astype(BF16)
    total = before_refs[0][...] if before_refs else None
    for slab, table_ref in enumerate(table_refs):
        of_atom = jnp.concatenate(list(atom_hits(ids_ref, place_ref, slab, pieces_of(half_index))), axis=0)
        for group in range(slots // GROUP):
            rows = slice(group * GROUP, (group + 1) * GROUP)
            picked = slice(slab * slots + group * GROUP, slab * slots + (group + 1) * GROUP)
            picks = jnp.concatenate([picks_of[band, picked, :] for band in range(bands)], axis=0)
            values = jnp.concatenate([jnp.where(low, picks, none), jnp.where(low, none, picks)], axis=0)
            tables = jnp.concatenate([table_ref[rows, t * LANES : (t + 1) * LANES] for t in range(pair_count)], axis=0)
            crossed = dot(tables, values, ((1,), (1,)))
            for t in range(pair_count):
                kept = jnp.where(diagonal, crossed[t * GROUP : (t + 1) * GROUP], 0.0)
                highs[rows, t * wide : (t + 1) * wide], rests[rows, t * wide : (t + 1) * wide] = two_terms(kept)
        slot_coef = dot(highs[...], gather_lanes) + dot(rests[...], gather_lanes)
        high, rest = two_terms(slot_coef)
        summed = dot(high, of_atom, ((0,), (0,))) + dot(rest, of_atom, ((0,), (0,)))
        total = summed if total is None else total + summed
    coef_ref[...] = total


def project(place, ids, tables, picks, projectors, padded, half_index, before):
    bands = len(picks)
    slots = tables[0].shape[0]
    width = projectors * bands * GROUP

    def kernel(place_ref, ids_ref, own_ref, other_ref, *rest):
        ends = [bands, bands + len(before)]
        project_kernel(
            projectors, padded, half_index, place_ref, ids_ref, (own_ref, other_ref),
            rest[: ends[0]], rest[ends[0] : ends[1]], *rest[ends[1] :],
        )

    return pl.pallas_call(
        kernel,
        in_specs=[SMEM_SPEC] + [VMEM_SPEC] * (3 + bands + len(before)),
        out_specs=VMEM_SPEC,
        out_shape=jax.ShapeDtypeStruct((bands * padded, LANES), F32),
        scratch_shapes=[pltpu.VMEM((bands, CORES * slots, LANES), BF16)] + [pltpu.VMEM((slots, width), BF16)] * 2,
        cost_estimate=pl.CostEstimate(flops=0, bytes_accessed=PROJECT_BYTES, transcendentals=0),
        compiler_params=PARAMS,
    )(place, ids, *tables, *picks, *before)


def apply_kernel(wanted, projectors, padded, place_ref, ids_ref, table_refs, count_ref, strength_ref, coef_refs, out_refs, wide_refs):
    pair_count = projectors // 2
    width = projectors * LANES // 2
    atom_total = strength_ref.shape[2]
    half = LANES // 2
    low = iota((half, LANES), 1) < half
    valid = (iota((projectors, atom_total), 0) < count_ref[...]).astype(F32)
    spread = (iota((projectors, width), 0) == iota((projectors, width), 1) // half).astype(BF16)
    for band, wide_ref in zip(wanted, wide_refs):
        total = coef_refs[0][band * padded : band * padded + projectors, :]
        for away in range(1, PARTNERS):
            first = (band ^ away) * padded
            total = total + coef_refs[away][first : first + projectors, :]
        total = total * valid
        coupled = strength_ref[:, 0, :] * total[0:1]
        for q in range(1, projectors):
            coupled = coupled + strength_ref[:, q, :] * total[q : q + 1]
        scaled = (coupled * valid).astype(BF16)
        wide_ref[...] = dot(scaled, spread, ((0,), (0,))).astype(BF16)
    for slab in range(CORES):
        for half_index in range(HALVES):
            table_ref = table_refs[half_index * CORES + slab]
            blocks = table_ref.shape[0] // LANES
            for i, of_atom in enumerate(atom_hits(ids_ref, place_ref, slab, pieces_of(half_index))):
                rows = slice(i * LANES, (i + 1) * LANES)
                first = ((slab * HALVES + half_index) * blocks + i) * half
                for wide_ref, out_ref in zip(wide_refs, out_refs):
                    total = None
                    for t in range(pair_count):
                        tile = slice(t * LANES, (t + 1) * LANES)
                        term = dot(of_atom, wide_ref[:, tile]) * table_ref[rows, tile].astype(F32)
                        total = term if total is None else total + term
                    total = total + pltpu.roll(total, half, 1)
                    packed = jnp.where(low, total[:half], total[half:])
                    out_ref[first : first + half, :] = packed.astype(BF16)


def back_project(wanted, place, ids, tables, count, strength, coefs, projectors, padded):
    slots = sum(table.shape[0] for table in tables)
    atom_total = strength.shape[2]

    def kernel(place_ref, ids_ref, count_ref, strength_ref, *rest):
        ends = [len(tables), len(tables) + len(coefs), len(tables) + len(coefs) + len(wanted)]
        apply_kernel(
            wanted, projectors, padded, place_ref, ids_ref, rest[: ends[0]], count_ref, strength_ref,
            rest[ends[0] : ends[1]], rest[ends[1] : ends[2]], rest[ends[2] :],
        )

    return pl.pallas_call(
        kernel,
        in_specs=[SMEM_SPEC] + [VMEM_SPEC] * (3 + len(tables) + len(coefs)),
        out_specs=[VMEM_SPEC] * len(wanted),
        out_shape=[jax.ShapeDtypeStruct((slots // 2, LANES), BF16)] * len(wanted),
        scratch_shapes=[pltpu.VMEM((atom_total, projectors * LANES // 2), BF16)] * len(wanted),
        compiler_params=PARAMS,
    )(place, ids, count, strength, *tables, *coefs)


def place_kernel(chips, wanted, place_ref, *refs):
    ids_ref, value_refs, out_ref = refs[0], dict(zip(wanted, refs[1:])), refs[-1]
    step = pl.program_id(0)
    half = LANES // 2
    rows = out_ref.shape[1] // LANES // CORES
    low = iota((half, LANES), 1) < half
    for number, chip in enumerate(chips):

        @pl.when(step == number)
        def _(chip=chip):
            for slab in range(CORES):
                place = place_ref[0] if slab == 0 else CORES - 1 - place_ref[0]
                parts, wanted = [], []
                for column in range(PARTNERS):
                    partner, piece = owner(chip, column)
                    ids = slot_ids(ids_ref, place_ref, slab, chip, column, 0)
                    for i, blocks in enumerate(ids):
                        wanted.append(jnp.right_shift(blocks, 1))
                        odd = jnp.bitwise_and(down(blocks), 1) == 1
                        first = ((slab * PIECES + piece) * len(ids) + i) * half
                        value = value_refs[partner][first : first + half, :].astype(F32)
                        turned = pltpu.roll(value, half, 1)
                        odd_a, odd_b = odd[:half], odd[half:]
                        part_a = jnp.where(odd_a, turned, value)
                        part_b = jnp.where(odd_b, value, turned)
                        parts.append(jnp.where(low != odd_a, part_a, 0.0).astype(BF16))
                        parts.append(jnp.where(low != odd_b, part_b, 0.0).astype(BF16))
                values = jnp.concatenate(parts, axis=0)
                wanted = jnp.concatenate(wanted, axis=1)
                start = place * rows * LANES
                for t in range(rows // LANES):
                    hits = (iota((LANES, wanted.shape[1]), 0) + t * LANES == wanted).astype(BF16)
                    total = dot(hits, values).astype(BF16)
                    for i in range(LANES // 16):
                        at = pl.multiple_of(start + t * LANES * LANES + i * 2048, 2048)
                        out_ref[0:1, pl.ds(at, 2048)] = total[i * 16 : (i + 1) * 16].reshape(1, 2048)


def place_rows(chips, place, ids, values, points, before):
    share = points // CHIPS
    wanted = tuple(values)
    small = (ids, *values.values())
    apart = chips[1] ^ chips[0]
    return pl.pallas_call(
        functools.partial(place_kernel, chips, wanted),
        grid_spec=pltpu.PrefetchScalarGridSpec(
            num_scalar_prefetch=1,
            grid=(len(chips),),
            in_specs=[pl.BlockSpec(x.shape, lambda i, place, rank=x.ndim: (0,) * rank) for x in small]
            + [pl.BlockSpec(memory_space=pl.ANY)] * len(before),
            out_specs=pl.BlockSpec((1, share), lambda i, place: (0, jnp.bitwise_xor(place[2], chips[0] + i * apart))),
        ),
        out_shape=jax.ShapeDtypeStruct((1, points), BF16),
        input_output_aliases={1 + len(small): 0} if before else {},
        compiler_params=PARAMS,
    )(place, *small, *before)


def body(columns, slabs, psi, beta, pair_atom, pair_block, proj_count, strength):
    atom_total, projectors = strength.shape[:2]
    padded = -(-projectors // 8) * 8
    position = lax.axis_index("slab").astype(jnp.int32)
    place = jnp.stack([lax.rem(position, CORES), lax.axis_index("band").astype(jnp.int32), position // CORES])

    def exchange(x, chip=0, column=0, core=0):
        turned = chip * CORES + core
        if column == 0:
            return lax.ppermute(x, "slab", [(i, i ^ turned) for i in range(slabs)])
        if turned == 0:
            return lax.ppermute(x, "band", [(i, i ^ column) for i in range(columns)])
        pairs = [(i, i ^ (column * slabs + turned)) for i in range(columns * slabs)]
        return lax.ppermute(x, ("band", "slab"), pairs)

    def partners(parts):
        return [parts[0]] + [exchange(parts[i], chip=i & 1, column=i & 2) for i in range(1, PARTNERS)]

    ids = jnp.concatenate([pair_block, pair_atom], axis=0).reshape(1, -1, LANES)
    ids = lax.all_to_all(jnp.broadcast_to(ids, (slabs, *ids.shape[1:])), "slab", 0, 0, tiled=True)
    rows = to_rows(psi)
    beside = exchange(beta[0], column=1)
    above = exchange(beta[0], chip=2)
    corner = exchange(above, column=1)
    picks = gather(place, ids, rows)
    shape = (projectors, padded)
    first = jnp.concatenate([after(table, picks[0]) for table in (beta[0], beside)], axis=0)
    picks = partners(picks)
    first = (first, exchange(first, core=1))
    coef = project(place, ids, first, picks, *shape, 0, ())
    second = jnp.concatenate([after(table, *picks[1:]) for table in (above, corner)], axis=0)
    second = (second, exchange(second, core=1))
    coef = project(place, ids, second, picks, *shape, 1, (coef,))
    coefs = partners([coef] * PARTNERS)
    count, strength = proj_count.reshape(1, atom_total), strength.transpose(1, 2, 0)
    given = (place, ids, first + second, count, strength, coefs, *shape)
    outer = back_project((3, 1), *given)
    inner = back_project((2, 0), *given)
    results = partners([inner[1], outer[1], inner[0], outer[0]])
    applied = place_rows((1, 3), place, ids, {1: results[1], 3: results[3]}, psi.shape[1], ())
    return place_rows((0, 2), place, ids, {0: results[0], 2: results[2]}, psi.shape[1], (applied,))


def plain_project(grid_blocks, tables, atom_ids, block_ids, atom_total):
    picked = jnp.take(grid_blocks, block_ids, axis=1)
    products = jnp.einsum("bkg,kpg->kpb", picked, tables, preferred_element_type=jnp.float32)
    slot_total = products.shape[0]
    onehot = (atom_ids[None, :] == jnp.arange(atom_total, dtype=jnp.int32)[:, None]).astype(
        jnp.float32
    )
    summed = jnp.dot(onehot, products.reshape(slot_total, -1), precision=lax.Precision.HIGHEST)
    return summed.reshape(atom_total, products.shape[1], products.shape[2])


def apply_strength(coef_total, strength, proj_valid):
    masked = coef_total * proj_valid[:, :, None]
    coupled = jnp.einsum("apq,aqb->apb", strength, masked, precision=lax.Precision.HIGHEST)
    return (coupled * proj_valid[:, :, None]).astype(jnp.bfloat16)


def plain_back_project(scaled, tables, atom_ids, block_ids, block_total):
    padded = jnp.concatenate([scaled, jnp.zeros((1,) + scaled.shape[1:], jnp.bfloat16)], axis=0)
    picked = jnp.take(padded, atom_ids, axis=0)
    products = jnp.einsum("kpg,kpb->kbg", tables, picked, preferred_element_type=jnp.float32)
    summed = jax.ops.segment_sum(products, block_ids, num_segments=block_total)
    band_rows = summed.shape[1]
    return summed.transpose(1, 0, 2).reshape(band_rows, -1).astype(jnp.bfloat16)


def plain_body(psi, beta, pair_atom, pair_block, proj_count, strength):
    atom_total = strength.shape[0]
    proj_total = strength.shape[1]
    block_size = beta.shape[2] // proj_total
    proj_valid = (jnp.arange(proj_total, dtype=jnp.int32)[None, :] < proj_count[:, None]).astype(
        jnp.float32
    )
    slab_tables = lax.all_gather(beta, "band", axis=1, tiled=True)
    slot_count = slab_tables.shape[1]
    slab_rows = lax.all_to_all(psi, "slab", split_axis=1, concat_axis=0, tiled=True)
    group_rows = slab_rows.shape[0]
    block_local = slab_rows.shape[1] // block_size
    grid_blocks = slab_rows.reshape(group_rows, block_local, block_size)
    tables = slab_tables.reshape(slot_count, proj_total, block_size)
    atom_ids = pair_atom.reshape(slot_count)
    block_ids = pair_block.reshape(slot_count)
    coef_part = plain_project(grid_blocks, tables, atom_ids, block_ids, atom_total)
    coef_total = lax.psum(coef_part, "slab")
    scaled = apply_strength(coef_total, strength, proj_valid)
    slab_applied = plain_back_project(scaled, tables, atom_ids, block_ids, block_local)
    return lax.all_to_all(slab_applied, "slab", split_axis=0, concat_axis=1, tiled=True)


def solution(mesh):
    placed = (
        P(("band", "slab"), None),
        P("slab", "band", None),
        P("slab", None),
        P("slab", None),
        P(),
        P(),
    )
    columns, slabs = mesh.shape["band"], mesh.shape["slab"]

    def chosen(*args):
        if (columns, slabs) == (PARTNERS, CORES * CHIPS) and args[1].shape[1] % LANES == 0:
            return body(columns, slabs, *args)
        return plain_body(*args)

    return jax.shard_map(
        chosen,
        mesh=mesh,
        in_specs=placed,
        out_specs=P(("band", "slab"), None),
        check_vma=False,
    )
```

```python
import functools

import jax
import jax.numpy as jnp
from jax import lax
from jax.experimental import pallas as pl
from jax.experimental.pallas import tpu as pltpu
from jax.sharding import PartitionSpec as P

CORES = 2
LANES = 128
CHIPS = 4
PARTNERS = 4
PIECES = 4
GROUP = 16
HALVES = 2
GATHER_BYTES = 10_000_000
PROJECT_BYTES = 30_000_000
F32 = jnp.float32
BF16 = jnp.bfloat16
VMEM_SPEC = pl.BlockSpec(memory_space=pltpu.VMEM)
SMEM_SPEC = pl.BlockSpec(memory_space=pltpu.SMEM)
PARAMS = pltpu.CompilerParams(vmem_limit_bytes=40 * 1024 * 1024)


def dot(a, b, contract=((1,), (0,))):
    return lax.dot_general(a, b, (contract, ((), ())), preferred_element_type=F32)


def two_terms(x):
    high = x.astype(BF16)
    return high, (x - high.astype(F32)).astype(BF16)


def after(x, *others):
    return lax.optimization_barrier((x, *others))[0]


def iota(shape, axis):
    return lax.broadcasted_iota(jnp.int32, shape, axis)


def slab_index(place_ref, turned, slab):
    core = place_ref[0] if slab == 0 else CORES - 1 - place_ref[0]
    return jnp.bitwise_xor(place_ref[2], turned) * CORES + core


def owner(turned_chip, turned_column):
    return (turned_chip & 1) | (turned_column & 2), (turned_chip & 2) | (turned_column & 1)


def pieces_of(half_index):
    return range(half_index * PIECES // HALVES, (half_index + 1) * PIECES // HALVES)


def slot_ids(ids_ref, place_ref, turned_chip, turned_column, kind):
    slot_rows = ids_ref.shape[1] // 2
    share = slot_rows // PARTNERS
    first = kind * slot_rows + jnp.bitwise_xor(place_ref[1], turned_column) * share
    return [ids_ref[turned_chip, pl.ds(first + i, 1), :] for i in range(share)]


def atom_hits(ids_ref, place_ref, pieces):
    lane = iota((LANES, LANES), 1)
    for piece in pieces:
        for atoms in slot_ids(ids_ref, place_ref, piece & 2, piece & 1, 1):
            yield (down(atoms) == lane).astype(BF16)


def down(ids):
    return jnp.transpose(jnp.broadcast_to(ids, (LANES, LANES)))


def rows_kernel(psi_ref, out_ref):
    def move(i, carry):
        part = psi_ref[0:1, pl.ds(pl.multiple_of(i * 2048, 2048), 2048)]
        out_ref[pl.ds(pl.multiple_of(i * 16, 16), 16), :] = part.reshape(16, LANES)
        return carry

    lax.fori_loop(0, out_ref.shape[0] // 16, move, 0, unroll=8)


def to_rows(psi):
    rows = psi.shape[1] // LANES
    return pl.pallas_call(
        rows_kernel,
        in_specs=[VMEM_SPEC],
        out_specs=VMEM_SPEC,
        out_shape=jax.ShapeDtypeStruct((rows, LANES), BF16),
        compiler_params=PARAMS,
    )(psi)


def gather_kernel(place_ref, ids_refs, rows_ref, out_refs):
    half = LANES // 2
    slab_rows = rows_ref.shape[0] // (CORES * CHIPS)
    lane = iota((LANES, LANES), 1)
    low = iota((half, LANES), 1) < half
    for chip in range(CHIPS):
        for slab in range(CORES):
            index = slab_index(place_ref, chip, slab)
            odds, hits, places = [], [], []
            for column in range(PARTNERS):
                partner, piece = owner(chip, column)
                ids = slot_ids(ids_refs[slab], place_ref, chip, column, 0)
                for i, row in enumerate(ids):
                    blocks = down(row)
                    wanted = jnp.right_shift(blocks, 1)
                    odds.append(jnp.bitwise_and(blocks, 1) == 1)
                    hits.append(
                        jnp.concatenate([(wanted - t * LANES == lane).astype(BF16) for t in range(slab_rows // LANES)], axis=1)
                    )
                    places.append((out_refs[partner], ((slab * PIECES + piece) * len(ids) + i) * half))
            first_row = pl.multiple_of(index * slab_rows, slab_rows)
            picked = dot(jnp.concatenate(hits, axis=0), rows_ref[pl.ds(first_row, slab_rows), :])
            for i, (odd, (out_ref, first)) in enumerate(zip(odds, places)):
                straight = picked[i * LANES : (i + 1) * LANES]
                turned = pltpu.roll(straight, half, 1)
                lower = jnp.where(odd, turned, straight)[:half]
                upper = jnp.where(odd, straight, turned)[half:]
                out_ref[first : first + half, :] = jnp.where(low, lower, upper).astype(BF16)


def gather(place, ids, rows):
    slots = CORES * PIECES * ids[0].shape[1] // 2 * LANES // PARTNERS

    def kernel(place_ref, own_ids, other_ids, rows_ref, *out_refs):
        gather_kernel(place_ref, (own_ids, other_ids), rows_ref, out_refs)

    return pl.pallas_call(
        kernel,
        in_specs=[SMEM_SPEC] + [VMEM_SPEC] * 3,
        out_specs=[VMEM_SPEC] * PARTNERS,
        out_shape=[jax.ShapeDtypeStruct((slots // 2, LANES), BF16)] * PARTNERS,
        cost_estimate=pl.CostEstimate(flops=0, bytes_accessed=GATHER_BYTES, transcendentals=0),
        compiler_params=PARAMS,
    )(place, *ids, rows)


def project_kernel(projectors, padded, half_index, place_ref, ids_refs, table_refs, packed_refs, before_refs, coef_ref, picks_of, terms):
    bands = len(packed_refs)
    slots = table_refs[0].shape[0]
    pair_count = projectors // 2
    wide = 2 * bands * GROUP
    low = iota((bands * GROUP, LANES), 1) < LANES // 2
    source = iota((pair_count * wide, bands * padded), 0) // GROUP
    target = iota((pair_count * wide, bands * padded), 1)
    gather_lanes = (target == lax.rem(source, bands) * padded + source // bands).astype(BF16)
    diagonal = lax.rem(iota((GROUP, wide), 0), GROUP) == lax.rem(iota((GROUP, wide), 1), GROUP)
    none = jnp.zeros((bands * GROUP, LANES), BF16)
    half = LANES // 2
    left = iota((half, LANES), 1) < half
    for band, packed_ref in enumerate(packed_refs):
        for i in range(CORES * slots // LANES):
            slab, block = divmod(i, slots // LANES)
            first = ((slab * HALVES + half_index) * (slots // LANES) + block) * half
            straight = packed_ref[first : first + half, :].astype(F32)
            turned = pltpu.roll(straight, half, 1)
            picks_of[band, i * LANES : i * LANES + half, :] = jnp.where(left, straight, turned).astype(BF16)
            picks_of[band, i * LANES + half : (i + 1) * LANES, :] = jnp.where(left, turned, straight).astype(BF16)
    of_atom = []
    for slab, table_ref in enumerate(table_refs):
        of_atom += atom_hits(ids_refs[slab], place_ref, pieces_of(half_index))
        for group in range(slots // GROUP):
            rows = slice(group * GROUP, (group + 1) * GROUP)
            first = slab * slots + group * GROUP
            high_rows, rest_rows = slice(first, first + GROUP), slice(CORES * slots + first, CORES * slots + first + GROUP)
            picks = jnp.concatenate([picks_of[band, high_rows, :] for band in range(bands)], axis=0)
            values = jnp.concatenate([jnp.where(low, picks, none), jnp.where(low, none, picks)], axis=0)
            tables = jnp.concatenate([table_ref[rows, t * LANES : (t + 1) * LANES] for t in range(pair_count)], axis=0)
            crossed = dot(tables, values, ((1,), (1,)))
            for t in range(pair_count):
                kept = jnp.where(diagonal, crossed[t * GROUP : (t + 1) * GROUP], 0.0)
                lanes = slice(t * wide, (t + 1) * wide)
                terms[high_rows, lanes], terms[rest_rows, lanes] = two_terms(kept)
    slot_coef = dot(terms[...], gather_lanes)
    high, rest = two_terms(slot_coef[: CORES * slots] + slot_coef[CORES * slots :])
    of_atom = jnp.concatenate(of_atom, axis=0)
    total = dot(high, of_atom, ((0,), (0,))) + dot(rest, of_atom, ((0,), (0,)))
    coef_ref[...] = total + before_refs[0][...] if before_refs else total


def project(place, ids, tables, picks, projectors, padded, half_index, before):
    bands = len(picks)
    slots = tables[0].shape[0]
    width = projectors * bands * GROUP

    def kernel(place_ref, own_ids, other_ids, own_ref, other_ref, *rest):
        ends = [bands, bands + len(before)]
        project_kernel(
            projectors, padded, half_index, place_ref, (own_ids, other_ids), (own_ref, other_ref),
            rest[: ends[0]], rest[ends[0] : ends[1]], *rest[ends[1] :],
        )

    return pl.pallas_call(
        kernel,
        in_specs=[SMEM_SPEC] + [VMEM_SPEC] * (4 + bands + len(before)),
        out_specs=VMEM_SPEC,
        out_shape=jax.ShapeDtypeStruct((bands * padded, LANES), F32),
        scratch_shapes=[pltpu.VMEM((bands, CORES * slots, LANES), BF16)] + [pltpu.VMEM((2 * CORES * slots, width), BF16)],
        cost_estimate=pl.CostEstimate(flops=0, bytes_accessed=PROJECT_BYTES, transcendentals=0),
        compiler_params=PARAMS,
    )(place, *ids, *tables, *picks, *before)


def apply_kernel(wanted, projectors, padded, place_ref, ids_refs, table_refs, count_ref, strength_ref, coef_refs, out_refs, wide_refs):
    pair_count = projectors // 2
    width = projectors * LANES // 2
    atom_total = strength_ref.shape[2]
    half = LANES // 2
    low = iota((half, LANES), 1) < half
    valid = (iota((projectors, atom_total), 0) < count_ref[...]).astype(F32)
    spread = (iota((projectors, width), 0) == iota((projectors, width), 1) // half).astype(BF16)
    for band, wide_ref in zip(wanted, wide_refs):
        total = coef_refs[0][band * padded : band * padded + projectors, :]
        for away in range(1, PARTNERS):
            first = (band ^ away) * padded
            total = total + coef_refs[away][first : first + projectors, :]
        total = total * valid
        coupled = strength_ref[:, 0, :] * total[0:1]
        for q in range(1, projectors):
            coupled = coupled + strength_ref[:, q, :] * total[q : q + 1]
        scaled = (coupled * valid).astype(BF16)
        wide_ref[...] = dot(scaled, spread, ((0,), (0,))).astype(BF16)
    for slab in range(CORES):
        for half_index in range(HALVES):
            table_ref = table_refs[half_index * CORES + slab]
            blocks = table_ref.shape[0] // LANES
            for i, of_atom in enumerate(atom_hits(ids_refs[slab], place_ref, pieces_of(half_index))):
                rows = slice(i * LANES, (i + 1) * LANES)
                first = ((slab * HALVES + half_index) * blocks + i) * half
                for wide_ref, out_ref in zip(wide_refs, out_refs):
                    total = None
                    for t in range(pair_count):
                        tile = slice(t * LANES, (t + 1) * LANES)
                        term = dot(of_atom, wide_ref[:, tile]) * table_ref[rows, tile].astype(F32)
                        total = term if total is None else total + term
                    total = total + pltpu.roll(total, half, 1)
                    packed = jnp.where(low, total[:half], total[half:])
                    out_ref[first : first + half, :] = packed.astype(BF16)


def back_project(wanted, place, ids, tables, count, strength, coefs, projectors, padded):
    slots = sum(table.shape[0] for table in tables)
    atom_total = strength.shape[2]

    def kernel(place_ref, own_ids, other_ids, count_ref, strength_ref, *rest):
        ends = [len(tables), len(tables) + len(coefs), len(tables) + len(coefs) + len(wanted)]
        apply_kernel(
            wanted, projectors, padded, place_ref, (own_ids, other_ids), rest[: ends[0]], count_ref, strength_ref,
            rest[ends[0] : ends[1]], rest[ends[1] : ends[2]], rest[ends[2] :],
        )

    return pl.pallas_call(
        kernel,
        in_specs=[SMEM_SPEC] + [VMEM_SPEC] * (4 + len(tables) + len(coefs)),
        out_specs=[VMEM_SPEC] * len(wanted),
        out_shape=[jax.ShapeDtypeStruct((slots // 2, LANES), BF16)] * len(wanted),
        scratch_shapes=[pltpu.VMEM((atom_total, projectors * LANES // 2), BF16)] * len(wanted),
        compiler_params=PARAMS,
    )(place, *ids, count, strength, *tables, *coefs)


def place_kernel(chips, wanted, place_ref, *refs):
    ids_refs, value_refs, out_ref = refs[:CORES], dict(zip(wanted, refs[CORES:])), refs[-1]
    step = pl.program_id(0)
    half = LANES // 2
    rows = out_ref.shape[1] // LANES // CORES
    low = iota((half, LANES), 1) < half
    for number, chip in enumerate(chips):

        @pl.when(step == number)
        def _(chip=chip):
            for slab in range(CORES):
                place = place_ref[0] if slab == 0 else CORES - 1 - place_ref[0]
                parts, wanted = [], []
                for column in range(PARTNERS):
                    partner, piece = owner(chip, column)
                    ids = slot_ids(ids_refs[slab], place_ref, chip, column, 0)
                    for i, blocks in enumerate(ids):
                        wanted.append(jnp.right_shift(blocks, 1))
                        odd = jnp.bitwise_and(down(blocks), 1) == 1
                        first = ((slab * PIECES + piece) * len(ids) + i) * half
                        value = value_refs[partner][first : first + half, :].astype(F32)
                        turned = pltpu.roll(value, half, 1)
                        odd_a, odd_b = odd[:half], odd[half:]
                        part_a = jnp.where(odd_a, turned, value)
                        part_b = jnp.where(odd_b, value, turned)
                        parts.append(jnp.where(low != odd_a, part_a, 0.0).astype(BF16))
                        parts.append(jnp.where(low != odd_b, part_b, 0.0).astype(BF16))
                values = jnp.concatenate(parts, axis=0)
                wanted = jnp.concatenate(wanted, axis=1)
                start = place * rows * LANES
                for t in range(rows // LANES):
                    hits = (iota((LANES, wanted.shape[1]), 0) + t * LANES == wanted).astype(BF16)
                    total = dot(hits, values).astype(BF16)
                    for i in range(LANES // 16):
                        at = pl.multiple_of(start + t * LANES * LANES + i * 2048, 2048)
                        out_ref[0:1, pl.ds(at, 2048)] = total[i * 16 : (i + 1) * 16].reshape(1, 2048)


def place_rows(chips, place, ids, values, points, before):
    share = points // CHIPS
    wanted = tuple(values)
    small = (*ids, *values.values())
    apart = chips[1] ^ chips[0]
    return pl.pallas_call(
        functools.partial(place_kernel, chips, wanted),
        grid_spec=pltpu.PrefetchScalarGridSpec(
            num_scalar_prefetch=1,
            grid=(len(chips),),
            in_specs=[pl.BlockSpec(x.shape, lambda i, place, rank=x.ndim: (0,) * rank) for x in small]
            + [pl.BlockSpec(memory_space=pl.ANY)] * len(before),
            out_specs=pl.BlockSpec((1, share), lambda i, place: (0, jnp.bitwise_xor(place[2], chips[0] + i * apart))),
        ),
        out_shape=jax.ShapeDtypeStruct((1, points), BF16),
        input_output_aliases={1 + len(small): 0} if before else {},
        compiler_params=PARAMS,
    )(place, *small, *before)


def body(columns, slabs, psi, beta, pair_atom, pair_block, proj_count, strength):
    atom_total, projectors = strength.shape[:2]
    padded = -(-projectors // 8) * 8
    position = lax.axis_index("slab").astype(jnp.int32)
    place = jnp.stack([lax.rem(position, CORES), lax.axis_index("band").astype(jnp.int32), position // CORES])

    def exchange(x, chip=0, column=0, core=0):
        turned = chip * CORES + core
        if column == 0:
            return lax.ppermute(x, "slab", [(i, i ^ turned) for i in range(slabs)])
        if turned == 0:
            return lax.ppermute(x, "band", [(i, i ^ column) for i in range(columns)])
        pairs = [(i, i ^ (column * slabs + turned)) for i in range(columns * slabs)]
        return lax.ppermute(x, ("band", "slab"), pairs)

    def partners(parts):
        return [parts[0]] + [exchange(parts[i], chip=i & 1, column=i & 2) for i in range(1, PARTNERS)]

    ids = jnp.concatenate([pair_block, pair_atom], axis=0).reshape(1, -1, LANES)
    ids = jnp.concatenate([ids] + [exchange(ids, chip=chip) for chip in range(1, CHIPS)], axis=0)
    ids = (ids, exchange(ids, core=1))
    rows = to_rows(psi)
    beside = exchange(beta[0], column=1)
    above = exchange(beta[0], chip=2)
    corner = exchange(above, column=1)
    picks = gather(place, ids, rows)
    shape = (projectors, padded)
    first = jnp.concatenate([after(table, picks[0]) for table in (beta[0], beside)], axis=0)
    picks = partners(picks)
    first = (first, exchange(first, core=1))
    coef = project(place, ids, first, picks, *shape, 0, ())
    second = jnp.concatenate([after(table, *picks[1:]) for table in (above, corner)], axis=0)
    second = (second, exchange(second, core=1))
    coef = project(place, ids, second, picks, *shape, 1, (coef,))
    coefs = partners([coef] * PARTNERS)
    count, strength = proj_count.reshape(1, atom_total), strength.transpose(1, 2, 0)
    given = (place, ids, first + second, count, strength, coefs, *shape)
    outer = back_project((3, 1), *given)
    inner = back_project((2, 0), *given)
    results = partners([inner[1], outer[1], inner[0], outer[0]])
    applied = place_rows((1, 3), place, ids, {1: results[1], 3: results[3]}, psi.shape[1], ())
    return place_rows((0, 2), place, ids, {0: results[0], 2: results[2]}, psi.shape[1], (applied,))


def plain_project(grid_blocks, tables, atom_ids, block_ids, atom_total):
    picked = jnp.take(grid_blocks, block_ids, axis=1)
    products = jnp.einsum("bkg,kpg->kpb", picked, tables, preferred_element_type=jnp.float32)
    slot_total = products.shape[0]
    onehot = (atom_ids[None, :] == jnp.arange(atom_total, dtype=jnp.int32)[:, None]).astype(
        jnp.float32
    )
    summed = jnp.dot(onehot, products.reshape(slot_total, -1), precision=lax.Precision.HIGHEST)
    return summed.reshape(atom_total, products.shape[1], products.shape[2])


def apply_strength(coef_total, strength, proj_valid):
    masked = coef_total * proj_valid[:, :, None]
    coupled = jnp.einsum("apq,aqb->apb", strength, masked, precision=lax.Precision.HIGHEST)
    return (coupled * proj_valid[:, :, None]).astype(jnp.bfloat16)


def plain_back_project(scaled, tables, atom_ids, block_ids, block_total):
    padded = jnp.concatenate([scaled, jnp.zeros((1,) + scaled.shape[1:], jnp.bfloat16)], axis=0)
    picked = jnp.take(padded, atom_ids, axis=0)
    products = jnp.einsum("kpg,kpb->kbg", tables, picked, preferred_element_type=jnp.float32)
    summed = jax.ops.segment_sum(products, block_ids, num_segments=block_total)
    band_rows = summed.shape[1]
    return summed.transpose(1, 0, 2).reshape(band_rows, -1).astype(jnp.bfloat16)


def plain_body(psi, beta, pair_atom, pair_block, proj_count, strength):
    atom_total = strength.shape[0]
    proj_total = strength.shape[1]
    block_size = beta.shape[2] // proj_total
    proj_valid = (jnp.arange(proj_total, dtype=jnp.int32)[None, :] < proj_count[:, None]).astype(
        jnp.float32
    )
    slab_tables = lax.all_gather(beta, "band", axis=1, tiled=True)
    slot_count = slab_tables.shape[1]
    slab_rows = lax.all_to_all(psi, "slab", split_axis=1, concat_axis=0, tiled=True)
    group_rows = slab_rows.shape[0]
    block_local = slab_rows.shape[1] // block_size
    grid_blocks = slab_rows.reshape(group_rows, block_local, block_size)
    tables = slab_tables.reshape(slot_count, proj_total, block_size)
    atom_ids = pair_atom.reshape(slot_count)
    block_ids = pair_block.reshape(slot_count)
    coef_part = plain_project(grid_blocks, tables, atom_ids, block_ids, atom_total)
    coef_total = lax.psum(coef_part, "slab")
    scaled = apply_strength(coef_total, strength, proj_valid)
    slab_applied = plain_back_project(scaled, tables, atom_ids, block_ids, block_local)
    return lax.all_to_all(slab_applied, "slab", split_axis=0, concat_axis=1, tiled=True)


def solution(mesh):
    placed = (
        P(("band", "slab"), None),
        P("slab", "band", None),
        P("slab", None),
        P("slab", None),
        P(),
        P(),
    )
    columns, slabs = mesh.shape["band"], mesh.shape["slab"]

    def chosen(*args):
        if (columns, slabs) == (PARTNERS, CORES * CHIPS) and args[1].shape[1] % LANES == 0:
            return body(columns, slabs, *args)
        return plain_body(*args)

    return jax.shard_map(
        chosen,
        mesh=mesh,
        in_specs=placed,
        out_specs=P(("band", "slab"), None),
        check_vma=False,
    )
```

```python
import functools

import jax
import jax.numpy as jnp
from jax import lax
from jax.experimental import pallas as pl
from jax.experimental.pallas import tpu as pltpu
from jax.sharding import PartitionSpec as P

CORES = 2
LANES = 128
CHIPS = 4
PARTNERS = 4
PIECES = 4
GROUP = 16
HALVES = 2
GATHER_BYTES = 10_000_000
PROJECT_BYTES = 30_000_000
F32 = jnp.float32
BF16 = jnp.bfloat16
VMEM_SPEC = pl.BlockSpec(memory_space=pltpu.VMEM)
PARAMS = pltpu.CompilerParams(vmem_limit_bytes=40 * 1024 * 1024)


def dot(a, b, contract=((1,), (0,))):
    return lax.dot_general(a, b, (contract, ((), ())), preferred_element_type=F32)


def two_terms(x):
    high = x.astype(BF16)
    return high, (x - high.astype(F32)).astype(BF16)


def after(x, *others):
    return lax.optimization_barrier((x, *others))[0]


def iota(shape, axis):
    return lax.broadcasted_iota(jnp.int32, shape, axis)


def own_place():
    position = lax.axis_index("slab")
    return jnp.bitwise_and(position, CORES - 1), lax.axis_index("band"), jnp.right_shift(position, 1)


def slab_index(place, turned, slab):
    core = place[0] if slab == 0 else CORES - 1 - place[0]
    return jnp.bitwise_xor(place[2], turned) * CORES + core


def owner(turned_chip, turned_column):
    return (turned_chip & 1) | (turned_column & 2), (turned_chip & 2) | (turned_column & 1)


def pieces_of(half_index):
    return range(half_index * PIECES // HALVES, (half_index + 1) * PIECES // HALVES)


def slot_ids(ids_ref, place, turned_chip, turned_column, kind):
    slot_rows = ids_ref.shape[1] // 2
    share = slot_rows // PARTNERS
    first = kind * slot_rows + jnp.bitwise_xor(place[1], turned_column) * share
    return [ids_ref[turned_chip, pl.ds(first + i, 1), :] for i in range(share)]


def atom_hits(ids_ref, place, pieces):
    lane = iota((LANES, LANES), 1)
    for piece in pieces:
        for atoms in slot_ids(ids_ref, place, piece & 2, piece & 1, 1):
            yield (down(atoms) == lane).astype(BF16)


def down(ids):
    return jnp.transpose(jnp.broadcast_to(ids, (LANES, LANES)))


def rows_kernel(psi_ref, out_ref):
    def move(i, carry):
        part = psi_ref[0:1, pl.ds(pl.multiple_of(i * 2048, 2048), 2048)]
        out_ref[pl.ds(pl.multiple_of(i * 16, 16), 16), :] = part.reshape(16, LANES)
        return carry

    lax.fori_loop(0, out_ref.shape[0] // 16, move, 0, unroll=8)


def to_rows(psi):
    rows = psi.shape[1] // LANES
    return pl.pallas_call(
        rows_kernel,
        in_specs=[VMEM_SPEC],
        out_specs=VMEM_SPEC,
        out_shape=jax.ShapeDtypeStruct((rows, LANES), BF16),
        compiler_params=PARAMS,
    )(psi)


def gather_kernel(ids_refs, rows_ref, out_refs):
    half = LANES // 2
    slab_rows = rows_ref.shape[0] // (CORES * CHIPS)
    lane = iota((LANES, LANES), 1)
    low = iota((half, LANES), 1) < half
    for chip in range(CHIPS):
        for slab in range(CORES):
            index = slab_index(own_place(), chip, slab)
            odds, hits, places = [], [], []
            for column in range(PARTNERS):
                partner, piece = owner(chip, column)
                ids = slot_ids(ids_refs[slab], own_place(), chip, column, 0)
                for i, row in enumerate(ids):
                    blocks = down(row)
                    wanted = jnp.right_shift(blocks, 1)
                    odds.append(jnp.bitwise_and(blocks, 1) == 1)
                    hits.append(
                        jnp.concatenate([(wanted - t * LANES == lane).astype(BF16) for t in range(slab_rows // LANES)], axis=1)
                    )
                    places.append((out_refs[partner], ((slab * PIECES + piece) * len(ids) + i) * half))
            first_row = pl.multiple_of(index * slab_rows, slab_rows)
            picked = dot(jnp.concatenate(hits, axis=0), rows_ref[pl.ds(first_row, slab_rows), :])
            for i, (odd, (out_ref, first)) in enumerate(zip(odds, places)):
                straight = picked[i * LANES : (i + 1) * LANES]
                turned = pltpu.roll(straight, half, 1)
                lower = jnp.where(odd, turned, straight)[:half]
                upper = jnp.where(odd, straight, turned)[half:]
                out_ref[first : first + half, :] = jnp.where(low, lower, upper).astype(BF16)


def gather(ids, rows):
    slots = CORES * PIECES * ids[0].shape[1] // 2 * LANES // PARTNERS

    def kernel(own_ids, other_ids, rows_ref, *out_refs):
        gather_kernel((own_ids, other_ids), rows_ref, out_refs)

    return pl.pallas_call(
        kernel,
        in_specs=[VMEM_SPEC] * 3,
        out_specs=[VMEM_SPEC] * PARTNERS,
        out_shape=[jax.ShapeDtypeStruct((slots // 2, LANES), BF16)] * PARTNERS,
        cost_estimate=pl.CostEstimate(flops=0, bytes_accessed=GATHER_BYTES, transcendentals=0),
        compiler_params=PARAMS,
    )(*ids, rows)


def project_kernel(projectors, padded, half_index, ids_refs, table_refs, packed_refs, before_refs, coef_ref, picks_of, terms):
    bands = len(packed_refs)
    slots = table_refs[0].shape[0]
    pair_count = projectors // 2
    wide = 2 * bands * GROUP
    low = iota((bands * GROUP, LANES), 1) < LANES // 2
    source = iota((pair_count * wide, bands * padded), 0) // GROUP
    target = iota((pair_count * wide, bands * padded), 1)
    gather_lanes = (target == lax.rem(source, bands) * padded + source // bands).astype(BF16)
    diagonal = lax.rem(iota((GROUP, wide), 0), GROUP) == lax.rem(iota((GROUP, wide), 1), GROUP)
    none = jnp.zeros((bands * GROUP, LANES), BF16)
    half = LANES // 2
    left = iota((half, LANES), 1) < half
    for band, packed_ref in enumerate(packed_refs):
        for i in range(CORES * slots // LANES):
            slab, block = divmod(i, slots // LANES)
            first = ((slab * HALVES + half_index) * (slots // LANES) + block) * half
            straight = packed_ref[first : first + half, :].astype(F32)
            turned = pltpu.roll(straight, half, 1)
            picks_of[band, i * LANES : i * LANES + half, :] = jnp.where(left, straight, turned).astype(BF16)
            picks_of[band, i * LANES + half : (i + 1) * LANES, :] = jnp.where(left, turned, straight).astype(BF16)
    of_atom = []
    for slab, table_ref in enumerate(table_refs):
        of_atom += atom_hits(ids_refs[slab], own_place(), pieces_of(half_index))
        for group in range(slots // GROUP):
            rows = slice(group * GROUP, (group + 1) * GROUP)
            first = slab * slots + group * GROUP
            high_rows, rest_rows = slice(first, first + GROUP), slice(CORES * slots + first, CORES * slots + first + GROUP)
            picks = jnp.concatenate([picks_of[band, high_rows, :] for band in range(bands)], axis=0)
            values = jnp.concatenate([jnp.where(low, picks, none), jnp.where(low, none, picks)], axis=0)
            tables = jnp.concatenate([table_ref[rows, t * LANES : (t + 1) * LANES] for t in range(pair_count)], axis=0)
            crossed = dot(tables, values, ((1,), (1,)))
            for t in range(pair_count):
                kept = jnp.where(diagonal, crossed[t * GROUP : (t + 1) * GROUP], 0.0)
                lanes = slice(t * wide, (t + 1) * wide)
                terms[high_rows, lanes], terms[rest_rows, lanes] = two_terms(kept)
    slot_coef = dot(terms[...], gather_lanes)
    high, rest = two_terms(slot_coef[: CORES * slots] + slot_coef[CORES * slots :])
    of_atom = jnp.concatenate(of_atom, axis=0)
    total = dot(high, of_atom, ((0,), (0,))) + dot(rest, of_atom, ((0,), (0,)))
    coef_ref[...] = total + before_refs[0][...] if before_refs else total


def project(ids, tables, picks, projectors, padded, half_index, before):
    bands = len(picks)
    slots = tables[0].shape[0]
    width = projectors * bands * GROUP

    def kernel(own_ids, other_ids, own_ref, other_ref, *rest):
        ends = [bands, bands + len(before)]
        project_kernel(
            projectors, padded, half_index, (own_ids, other_ids), (own_ref, other_ref),
            rest[: ends[0]], rest[ends[0] : ends[1]], *rest[ends[1] :],
        )

    return pl.pallas_call(
        kernel,
        in_specs=[VMEM_SPEC] * (4 + bands + len(before)),
        out_specs=VMEM_SPEC,
        out_shape=jax.ShapeDtypeStruct((bands * padded, LANES), F32),
        scratch_shapes=[pltpu.VMEM((bands, CORES * slots, LANES), BF16)] + [pltpu.VMEM((2 * CORES * slots, width), BF16)],
        cost_estimate=pl.CostEstimate(flops=0, bytes_accessed=PROJECT_BYTES, transcendentals=0),
        compiler_params=PARAMS,
    )(*ids, *tables, *picks, *before)


def apply_kernel(wanted, projectors, padded, ids_refs, table_refs, count_ref, strength_ref, coef_refs, out_refs, wide_refs):
    pair_count = projectors // 2
    width = projectors * LANES // 2
    atom_total = strength_ref.shape[2]
    half = LANES // 2
    low = iota((half, LANES), 1) < half
    valid = (iota((projectors, atom_total), 0) < count_ref[...]).astype(F32)
    spread = (iota((projectors, width), 0) == iota((projectors, width), 1) // half).astype(BF16)
    for band, wide_ref in zip(wanted, wide_refs):
        total = coef_refs[0][band * padded : band * padded + projectors, :]
        for away in range(1, PARTNERS):
            first = (band ^ away) * padded
            total = total + coef_refs[away][first : first + projectors, :]
        total = total * valid
        coupled = strength_ref[:, 0, :] * total[0:1]
        for q in range(1, projectors):
            coupled = coupled + strength_ref[:, q, :] * total[q : q + 1]
        scaled = (coupled * valid).astype(BF16)
        wide_ref[...] = dot(scaled, spread, ((0,), (0,))).astype(BF16)
    for slab in range(CORES):
        for half_index in range(HALVES):
            table_ref = table_refs[half_index * CORES + slab]
            blocks = table_ref.shape[0] // LANES
            for i, of_atom in enumerate(atom_hits(ids_refs[slab], own_place(), pieces_of(half_index))):
                rows = slice(i * LANES, (i + 1) * LANES)
                first = ((slab * HALVES + half_index) * blocks + i) * half
                for wide_ref, out_ref in zip(wide_refs, out_refs):
                    total = None
                    for t in range(pair_count):
                        tile = slice(t * LANES, (t + 1) * LANES)
                        term = dot(of_atom, wide_ref[:, tile]) * table_ref[rows, tile].astype(F32)
                        total = term if total is None else total + term
                    total = total + pltpu.roll(total, half, 1)
                    packed = jnp.where(low, total[:half], total[half:])
                    out_ref[first : first + half, :] = packed.astype(BF16)


def back_project(wanted, ids, tables, count, strength, coefs, projectors, padded):
    slots = sum(table.shape[0] for table in tables)
    atom_total = strength.shape[2]

    def kernel(own_ids, other_ids, count_ref, strength_ref, *rest):
        ends = [len(tables), len(tables) + len(coefs), len(tables) + len(coefs) + len(wanted)]
        apply_kernel(
            wanted, projectors, padded, (own_ids, other_ids), rest[: ends[0]], count_ref, strength_ref,
            rest[ends[0] : ends[1]], rest[ends[1] : ends[2]], rest[ends[2] :],
        )

    return pl.pallas_call(
        kernel,
        in_specs=[VMEM_SPEC] * (4 + len(tables) + len(coefs)),
        out_specs=[VMEM_SPEC] * len(wanted),
        out_shape=[jax.ShapeDtypeStruct((slots // 2, LANES), BF16)] * len(wanted),
        scratch_shapes=[pltpu.VMEM((atom_total, projectors * LANES // 2), BF16)] * len(wanted),
        compiler_params=PARAMS,
    )(*ids, count, strength, *tables, *coefs)


def place_kernel(chips, wanted, *refs):
    ids_refs, value_refs, out_ref = refs[:CORES], dict(zip(wanted, refs[CORES:])), refs[-1]
    step = pl.program_id(0)
    half = LANES // 2
    rows = out_ref.shape[1] // LANES // CORES
    low = iota((half, LANES), 1) < half
    for number, chip in enumerate(chips):

        @pl.when(step == number)
        def _(chip=chip):
            for slab in range(CORES):
                place = own_place()[0] if slab == 0 else CORES - 1 - own_place()[0]
                parts, wanted = [], []
                for column in range(PARTNERS):
                    partner, piece = owner(chip, column)
                    ids = slot_ids(ids_refs[slab], own_place(), chip, column, 0)
                    for i, blocks in enumerate(ids):
                        wanted.append(jnp.right_shift(blocks, 1))
                        odd = jnp.bitwise_and(down(blocks), 1) == 1
                        first = ((slab * PIECES + piece) * len(ids) + i) * half
                        value = value_refs[partner][first : first + half, :].astype(F32)
                        turned = pltpu.roll(value, half, 1)
                        odd_a, odd_b = odd[:half], odd[half:]
                        part_a = jnp.where(odd_a, turned, value)
                        part_b = jnp.where(odd_b, value, turned)
                        parts.append(jnp.where(low != odd_a, part_a, 0.0).astype(BF16))
                        parts.append(jnp.where(low != odd_b, part_b, 0.0).astype(BF16))
                values = jnp.concatenate(parts, axis=0)
                wanted = jnp.concatenate(wanted, axis=1)
                start = place * rows * LANES
                for t in range(rows // LANES):
                    hits = (iota((LANES, wanted.shape[1]), 0) + t * LANES == wanted).astype(BF16)
                    total = dot(hits, values).astype(BF16)
                    for i in range(LANES // 16):
                        at = pl.multiple_of(start + t * LANES * LANES + i * 2048, 2048)
                        out_ref[0:1, pl.ds(at, 2048)] = total[i * 16 : (i + 1) * 16].reshape(1, 2048)


def place_rows(chips, ids, values, points, before):
    share = points // CHIPS
    wanted = tuple(values)
    small = (*ids, *values.values())
    apart = chips[1] ^ chips[0]
    return pl.pallas_call(
        functools.partial(place_kernel, chips, wanted),
        grid=(len(chips),),
        in_specs=[pl.BlockSpec(x.shape, lambda i, rank=x.ndim: (0,) * rank) for x in small]
        + [pl.BlockSpec(memory_space=pl.ANY)] * len(before),
        out_specs=pl.BlockSpec((1, share), lambda i: (0, jnp.bitwise_xor(own_place()[2], chips[0] + i * apart))),
        out_shape=jax.ShapeDtypeStruct((1, points), BF16),
        input_output_aliases={len(small): 0} if before else {},
        compiler_params=PARAMS,
    )(*small, *before)


def body(columns, slabs, psi, beta, pair_atom, pair_block, proj_count, strength):
    atom_total, projectors = strength.shape[:2]
    padded = -(-projectors // 8) * 8

    def exchange(x, chip=0, column=0, core=0):
        turned = chip * CORES + core
        if column == 0:
            return lax.ppermute(x, "slab", [(i, i ^ turned) for i in range(slabs)])
        if turned == 0:
            return lax.ppermute(x, "band", [(i, i ^ column) for i in range(columns)])
        pairs = [(i, i ^ (column * slabs + turned)) for i in range(columns * slabs)]
        return lax.ppermute(x, ("band", "slab"), pairs)

    def partners(parts):
        return [parts[0]] + [exchange(parts[i], chip=i & 1, column=i & 2) for i in range(1, PARTNERS)]

    ids = jnp.concatenate([pair_block, pair_atom], axis=0).reshape(1, -1, LANES)
    ids = jnp.concatenate([ids] + [exchange(ids, chip=chip) for chip in range(1, CHIPS)], axis=0)
    ids = (ids, exchange(ids, core=1))
    rows = to_rows(psi)
    beside = exchange(beta[0], column=1)
    above = exchange(beta[0], chip=2)
    corner = exchange(above, column=1)
    picks = gather(ids, rows)
    shape = (projectors, padded)
    first = jnp.concatenate([after(table, picks[0]) for table in (beta[0], beside)], axis=0)
    picks = partners(picks)
    first = (first, exchange(first, core=1))
    coef = project(ids, first, picks, *shape, 0, ())
    second = jnp.concatenate([after(table, *picks[1:]) for table in (above, corner)], axis=0)
    second = (second, exchange(second, core=1))
    coef = project(ids, second, picks, *shape, 1, (coef,))
    coefs = partners([coef] * PARTNERS)
    count, strength = proj_count.reshape(1, atom_total), strength.transpose(1, 2, 0)
    given = (ids, first + second, count, strength, coefs, *shape)
    outer = back_project((3, 1), *given)
    inner = back_project((2, 0), *given)
    results = partners([inner[1], outer[1], inner[0], outer[0]])
    applied = place_rows((1, 3), ids, {1: results[1], 3: results[3]}, psi.shape[1], ())
    return place_rows((0, 2), ids, {0: results[0], 2: results[2]}, psi.shape[1], (applied,))


def plain_project(grid_blocks, tables, atom_ids, block_ids, atom_total):
    picked = jnp.take(grid_blocks, block_ids, axis=1)
    products = jnp.einsum("bkg,kpg->kpb", picked, tables, preferred_element_type=jnp.float32)
    slot_total = products.shape[0]
    onehot = (atom_ids[None, :] == jnp.arange(atom_total, dtype=jnp.int32)[:, None]).astype(
        jnp.float32
    )
    summed = jnp.dot(onehot, products.reshape(slot_total, -1), precision=lax.Precision.HIGHEST)
    return summed.reshape(atom_total, products.shape[1], products.shape[2])


def apply_strength(coef_total, strength, proj_valid):
    masked = coef_total * proj_valid[:, :, None]
    coupled = jnp.einsum("apq,aqb->apb", strength, masked, precision=lax.Precision.HIGHEST)
    return (coupled * proj_valid[:, :, None]).astype(jnp.bfloat16)


def plain_back_project(scaled, tables, atom_ids, block_ids, block_total):
    padded = jnp.concatenate([scaled, jnp.zeros((1,) + scaled.shape[1:], jnp.bfloat16)], axis=0)
    picked = jnp.take(padded, atom_ids, axis=0)
    products = jnp.einsum("kpg,kpb->kbg", tables, picked, preferred_element_type=jnp.float32)
    summed = jax.ops.segment_sum(products, block_ids, num_segments=block_total)
    band_rows = summed.shape[1]
    return summed.transpose(1, 0, 2).reshape(band_rows, -1).astype(jnp.bfloat16)


def plain_body(psi, beta, pair_atom, pair_block, proj_count, strength):
    atom_total = strength.shape[0]
    proj_total = strength.shape[1]
    block_size = beta.shape[2] // proj_total
    proj_valid = (jnp.arange(proj_total, dtype=jnp.int32)[None, :] < proj_count[:, None]).astype(
        jnp.float32
    )
    slab_tables = lax.all_gather(beta, "band", axis=1, tiled=True)
    slot_count = slab_tables.shape[1]
    slab_rows = lax.all_to_all(psi, "slab", split_axis=1, concat_axis=0, tiled=True)
    group_rows = slab_rows.shape[0]
    block_local = slab_rows.shape[1] // block_size
    grid_blocks = slab_rows.reshape(group_rows, block_local, block_size)
    tables = slab_tables.reshape(slot_count, proj_total, block_size)
    atom_ids = pair_atom.reshape(slot_count)
    block_ids = pair_block.reshape(slot_count)
    coef_part = plain_project(grid_blocks, tables, atom_ids, block_ids, atom_total)
    coef_total = lax.psum(coef_part, "slab")
    scaled = apply_strength(coef_total, strength, proj_valid)
    slab_applied = plain_back_project(scaled, tables, atom_ids, block_ids, block_local)
    return lax.all_to_all(slab_applied, "slab", split_axis=0, concat_axis=1, tiled=True)


def solution(mesh):
    placed = (
        P(("band", "slab"), None),
        P("slab", "band", None),
        P("slab", None),
        P("slab", None),
        P(),
        P(),
    )
    columns, slabs = mesh.shape["band"], mesh.shape["slab"]

    def chosen(*args):
        if (columns, slabs) == (PARTNERS, CORES * CHIPS) and args[1].shape[1] % LANES == 0:
            return body(columns, slabs, *args)
        return plain_body(*args)

    return jax.shard_map(
        chosen,
        mesh=mesh,
        in_specs=placed,
        out_specs=P(("band", "slab"), None),
        check_vma=False,
    )
```

```python
import functools

import jax
import jax.numpy as jnp
from jax import lax
from jax.experimental import pallas as pl
from jax.experimental.pallas import tpu as pltpu
from jax.sharding import PartitionSpec as P

CORES = 2
LANES = 128
CHIPS = 4
PARTNERS = 4
PIECES = 4
GROUP = 16
HALVES = 2
GATHER_BYTES = 10_000_000
PROJECT_BYTES = 30_000_000
F32 = jnp.float32
BF16 = jnp.bfloat16
VMEM_SPEC = pl.BlockSpec(memory_space=pltpu.VMEM)
PARAMS = pltpu.CompilerParams(vmem_limit_bytes=40 * 1024 * 1024)


def dot(a, b, contract=((1,), (0,))):
    return lax.dot_general(a, b, (contract, ((), ())), preferred_element_type=F32)


def two_terms(x):
    high = x.astype(BF16)
    return high, (x - high.astype(F32)).astype(BF16)


def after(x, *others):
    return lax.optimization_barrier((x, *others))[0]


def iota(shape, axis):
    return lax.broadcasted_iota(jnp.int32, shape, axis)


def own_place():
    position = lax.axis_index("slab")
    return jnp.bitwise_and(position, CORES - 1), lax.axis_index("band"), jnp.right_shift(position, 1)


def slab_index(place, turned, slab):
    core = place[0] if slab == 0 else CORES - 1 - place[0]
    return jnp.bitwise_xor(place[2], turned) * CORES + core


def owner(turned_chip, turned_column):
    return (turned_chip & 1) | (turned_column & 2), (turned_chip & 2) | (turned_column & 1)


def pieces_of(half_index):
    return range(half_index * PIECES // HALVES, (half_index + 1) * PIECES // HALVES)


def slot_ids(ids_ref, place, turned_chip, turned_column, kind):
    slot_rows = ids_ref.shape[1] // 2
    share = slot_rows // PARTNERS
    first = kind * slot_rows + jnp.bitwise_xor(place[1], turned_column) * share
    return [ids_ref[turned_chip, pl.ds(first + i, 1), :] for i in range(share)]


def atom_hits(ids_ref, place, pieces):
    lane = iota((LANES, LANES), 1)
    for piece in pieces:
        for atoms in slot_ids(ids_ref, place, piece & 2, piece & 1, 1):
            yield (down(atoms) == lane).astype(BF16)


def down(ids):
    return jnp.transpose(jnp.broadcast_to(ids, (LANES, LANES)))


def rows_kernel(psi_ref, out_ref):
    def move(i, carry):
        part = psi_ref[0:1, pl.ds(pl.multiple_of(i * 2048, 2048), 2048)]
        out_ref[pl.ds(pl.multiple_of(i * 16, 16), 16), :] = part.reshape(16, LANES)
        return carry

    lax.fori_loop(0, out_ref.shape[0] // 16, move, 0, unroll=8)


def to_rows(psi):
    rows = psi.shape[1] // LANES
    return pl.pallas_call(
        rows_kernel,
        in_specs=[VMEM_SPEC],
        out_specs=VMEM_SPEC,
        out_shape=jax.ShapeDtypeStruct((rows, LANES), BF16),
        compiler_params=PARAMS,
    )(psi)


def gather_kernel(ids_refs, rows_ref, out_refs):
    half = LANES // 2
    slab_rows = rows_ref.shape[0] // (CORES * CHIPS)
    lane = iota((LANES, LANES), 1)
    low = iota((half, LANES), 1) < half
    for chip in range(CHIPS):
        for slab in range(CORES):
            index = slab_index(own_place(), chip, slab)
            odds, hits, places = [], [], []
            for column in range(PARTNERS):
                partner, piece = owner(chip, column)
                ids = slot_ids(ids_refs[slab], own_place(), chip, column, 0)
                for i, row in enumerate(ids):
                    blocks = down(row)
                    wanted = jnp.right_shift(blocks, 1)
                    odds.append(jnp.bitwise_and(blocks, 1) == 1)
                    hits.append(
                        jnp.concatenate([(wanted - t * LANES == lane).astype(BF16) for t in range(slab_rows // LANES)], axis=1)
                    )
                    places.append((out_refs[partner], ((slab * PIECES + piece) * len(ids) + i) * half))
            first_row = pl.multiple_of(index * slab_rows, slab_rows)
            picked = dot(jnp.concatenate(hits, axis=0), rows_ref[pl.ds(first_row, slab_rows), :])
            for i, (odd, (out_ref, first)) in enumerate(zip(odds, places)):
                straight = picked[i * LANES : (i + 1) * LANES]
                turned = pltpu.roll(straight, half, 1)
                lower = jnp.where(odd, turned, straight)[:half]
                upper = jnp.where(odd, straight, turned)[half:]
                out_ref[first : first + half, :] = jnp.where(low, lower, upper).astype(BF16)


def gather(ids, rows):
    slots = CORES * PIECES * ids[0].shape[1] // 2 * LANES // PARTNERS

    def kernel(own_ids, other_ids, rows_ref, *out_refs):
        gather_kernel((own_ids, other_ids), rows_ref, out_refs)

    return pl.pallas_call(
        kernel,
        in_specs=[VMEM_SPEC] * 3,
        out_specs=[VMEM_SPEC] * PARTNERS,
        out_shape=[jax.ShapeDtypeStruct((slots // 2, LANES), BF16)] * PARTNERS,
        cost_estimate=pl.CostEstimate(flops=0, bytes_accessed=GATHER_BYTES, transcendentals=0),
        compiler_params=PARAMS,
    )(*ids, rows)


def project_kernel(projectors, padded, half_index, ids_refs, table_refs, packed_refs, before_refs, coef_ref, picks_of, terms):
    bands = len(packed_refs)
    slots = table_refs[0].shape[0]
    pair_count = projectors // 2
    wide = 2 * bands * GROUP
    low = iota((bands * GROUP, LANES), 1) < LANES // 2
    source = iota((pair_count * wide, bands * padded), 0) // GROUP
    target = iota((pair_count * wide, bands * padded), 1)
    gather_lanes = (target == lax.rem(source, bands) * padded + source // bands).astype(BF16)
    diagonal = lax.rem(iota((GROUP, wide), 0), GROUP) == lax.rem(iota((GROUP, wide), 1), GROUP)
    none = jnp.zeros((bands * GROUP, LANES), BF16)
    half = LANES // 2
    left = iota((half, LANES), 1) < half
    for band, packed_ref in enumerate(packed_refs):
        for i in range(CORES * slots // LANES):
            slab, block = divmod(i, slots // LANES)
            first = ((slab * HALVES + half_index) * (slots // LANES) + block) * half
            straight = packed_ref[first : first + half, :].astype(F32)
            turned = pltpu.roll(straight, half, 1)
            picks_of[band, i * LANES : i * LANES + half, :] = jnp.where(left, straight, turned).astype(BF16)
            picks_of[band, i * LANES + half : (i + 1) * LANES, :] = jnp.where(left, turned, straight).astype(BF16)
    of_atom = []
    for slab, table_ref in enumerate(table_refs):
        of_atom += atom_hits(ids_refs[slab], own_place(), pieces_of(half_index))
        for group in range(slots // GROUP):
            rows = slice(group * GROUP, (group + 1) * GROUP)
            first = slab * slots + group * GROUP
            high_rows, rest_rows = slice(first, first + GROUP), slice(CORES * slots + first, CORES * slots + first + GROUP)
            picks = jnp.concatenate([picks_of[band, high_rows, :] for band in range(bands)], axis=0)
            values = jnp.concatenate([jnp.where(low, picks, none), jnp.where(low, none, picks)], axis=0)
            tables = jnp.concatenate([table_ref[rows, t * LANES : (t + 1) * LANES] for t in range(pair_count)], axis=0)
            crossed = dot(tables, values, ((1,), (1,)))
            for t in range(pair_count):
                kept = jnp.where(diagonal, crossed[t * GROUP : (t + 1) * GROUP], 0.0)
                lanes = slice(t * wide, (t + 1) * wide)
                terms[high_rows, lanes], terms[rest_rows, lanes] = two_terms(kept)
    slot_coef = dot(terms[...], gather_lanes)
    high, rest = two_terms(slot_coef[: CORES * slots] + slot_coef[CORES * slots :])
    of_atom = jnp.concatenate(of_atom, axis=0)
    total = dot(high, of_atom, ((0,), (0,))) + dot(rest, of_atom, ((0,), (0,)))
    coef_ref[...] = total + before_refs[0][...] if before_refs else total


def project(ids, tables, picks, projectors, padded, half_index, before):
    bands = len(picks)
    slots = tables[0].shape[0]
    width = projectors * bands * GROUP

    def kernel(own_ids, other_ids, own_ref, other_ref, *rest):
        ends = [bands, bands + len(before)]
        project_kernel(
            projectors, padded, half_index, (own_ids, other_ids), (own_ref, other_ref),
            rest[: ends[0]], rest[ends[0] : ends[1]], *rest[ends[1] :],
        )

    return pl.pallas_call(
        kernel,
        in_specs=[VMEM_SPEC] * (4 + bands + len(before)),
        out_specs=VMEM_SPEC,
        out_shape=jax.ShapeDtypeStruct((bands * padded, LANES), F32),
        scratch_shapes=[pltpu.VMEM((bands, CORES * slots, LANES), BF16)] + [pltpu.VMEM((2 * CORES * slots, width), BF16)],
        cost_estimate=pl.CostEstimate(flops=0, bytes_accessed=PROJECT_BYTES, transcendentals=0),
        compiler_params=PARAMS,
    )(*ids, *tables, *picks, *before)


def apply_kernel(wanted, projectors, padded, ids_refs, table_refs, count_ref, strength_ref, coef_refs, out_refs, wide_refs):
    pair_count = projectors // 2
    width = projectors * LANES // 2
    atom_total = strength_ref.shape[2]
    half = LANES // 2
    low = iota((half, LANES), 1) < half
    valid = (iota((projectors, atom_total), 0) < count_ref[...]).astype(F32)
    spread = (iota((projectors, width), 0) == iota((projectors, width), 1) // half).astype(BF16)
    for band, wide_ref in zip(wanted, wide_refs):
        total = coef_refs[0][band * padded : band * padded + projectors, :]
        for away in range(1, PARTNERS):
            first = (band ^ away) * padded
            total = total + coef_refs[away][first : first + projectors, :]
        total = total * valid
        coupled = strength_ref[:, 0, :] * total[0:1]
        for q in range(1, projectors):
            coupled = coupled + strength_ref[:, q, :] * total[q : q + 1]
        scaled = (coupled * valid).astype(BF16)
        wide_ref[...] = dot(scaled, spread, ((0,), (0,))).astype(BF16)
    for slab in range(CORES):
        for half_index in range(HALVES):
            table_ref = table_refs[half_index * CORES + slab]
            blocks = table_ref.shape[0] // LANES
            for i, of_atom in enumerate(atom_hits(ids_refs[slab], own_place(), pieces_of(half_index))):
                rows = slice(i * LANES, (i + 1) * LANES)
                first = ((slab * HALVES + half_index) * blocks + i) * half
                for wide_ref, out_ref in zip(wide_refs, out_refs):
                    total = None
                    for t in range(pair_count):
                        tile = slice(t * LANES, (t + 1) * LANES)
                        term = dot(of_atom, wide_ref[:, tile]) * table_ref[rows, tile].astype(F32)
                        total = term if total is None else total + term
                    total = total + pltpu.roll(total, half, 1)
                    packed = jnp.where(low, total[:half], total[half:])
                    out_ref[first : first + half, :] = packed.astype(BF16)


def back_project(wanted, ids, tables, count, strength, coefs, projectors, padded):
    slots = sum(table.shape[0] for table in tables)
    atom_total = strength.shape[2]

    def kernel(own_ids, other_ids, count_ref, strength_ref, *rest):
        ends = [len(tables), len(tables) + len(coefs), len(tables) + len(coefs) + len(wanted)]
        apply_kernel(
            wanted, projectors, padded, (own_ids, other_ids), rest[: ends[0]], count_ref, strength_ref,
            rest[ends[0] : ends[1]], rest[ends[1] : ends[2]], rest[ends[2] :],
        )

    return pl.pallas_call(
        kernel,
        in_specs=[VMEM_SPEC] * (4 + len(tables) + len(coefs)),
        out_specs=[VMEM_SPEC] * len(wanted),
        out_shape=[jax.ShapeDtypeStruct((slots // 2, LANES), BF16)] * len(wanted),
        scratch_shapes=[pltpu.VMEM((atom_total, projectors * LANES // 2), BF16)] * len(wanted),
        compiler_params=PARAMS,
    )(*ids, count, strength, *tables, *coefs)


def place_kernel(chips, wanted, *refs):
    ids_refs, value_refs, out_ref = refs[:CORES], dict(zip(wanted, refs[CORES:])), refs[-1]
    step = pl.program_id(0)
    half = LANES // 2
    rows = out_ref.shape[1] // LANES // CORES
    low = iota((half, LANES), 1) < half
    for number, chip in enumerate(chips):

        @pl.when(step == number)
        def _(chip=chip):
            for slab in range(CORES):
                place = own_place()[0] if slab == 0 else CORES - 1 - own_place()[0]
                parts, wanted = [], []
                for column in range(PARTNERS):
                    partner, piece = owner(chip, column)
                    ids = slot_ids(ids_refs[slab], own_place(), chip, column, 0)
                    for i, blocks in enumerate(ids):
                        wanted.append(jnp.right_shift(blocks, 1))
                        odd = jnp.bitwise_and(down(blocks), 1) == 1
                        first = ((slab * PIECES + piece) * len(ids) + i) * half
                        value = value_refs[partner][first : first + half, :].astype(F32)
                        turned = pltpu.roll(value, half, 1)
                        odd_a, odd_b = odd[:half], odd[half:]
                        part_a = jnp.where(odd_a, turned, value)
                        part_b = jnp.where(odd_b, value, turned)
                        parts.append(jnp.where(low != odd_a, part_a, 0.0).astype(BF16))
                        parts.append(jnp.where(low != odd_b, part_b, 0.0).astype(BF16))
                values = jnp.concatenate(parts, axis=0)
                wanted = jnp.concatenate(wanted, axis=1)
                start = place * rows * LANES
                for t in range(rows // LANES):
                    hits = (iota((LANES, wanted.shape[1]), 0) + t * LANES == wanted).astype(BF16)
                    total = dot(hits, values).astype(BF16)
                    for i in range(LANES // 16):
                        at = pl.multiple_of(start + t * LANES * LANES + i * 2048, 2048)
                        out_ref[0:1, pl.ds(at, 2048)] = total[i * 16 : (i + 1) * 16].reshape(1, 2048)


def place_rows(chips, ids, values, points, before):
    share = points // CHIPS
    wanted = tuple(values)
    small = (*ids, *values.values())
    apart = chips[1] ^ chips[0]
    return pl.pallas_call(
        functools.partial(place_kernel, chips, wanted),
        grid=(len(chips),),
        in_specs=[pl.BlockSpec(x.shape, lambda i, rank=x.ndim: (0,) * rank) for x in small]
        + [pl.BlockSpec(memory_space=pl.ANY)] * len(before),
        out_specs=pl.BlockSpec((1, share), lambda i: (0, jnp.bitwise_xor(own_place()[2], chips[0] + i * apart))),
        out_shape=jax.ShapeDtypeStruct((1, points), BF16),
        input_output_aliases={len(small): 0} if before else {},
        compiler_params=PARAMS,
    )(*small, *before)


def body(columns, slabs, psi, beta, pair_atom, pair_block, proj_count, strength):
    atom_total, projectors = strength.shape[:2]
    padded = -(-projectors // 8) * 8

    def exchange(x, chip=0, column=0, core=0):
        turned = chip * CORES + core
        if column == 0:
            return lax.ppermute(x, "slab", [(i, i ^ turned) for i in range(slabs)])
        if turned == 0:
            return lax.ppermute(x, "band", [(i, i ^ column) for i in range(columns)])
        pairs = [(i, i ^ (column * slabs + turned)) for i in range(columns * slabs)]
        return lax.ppermute(x, ("band", "slab"), pairs)

    def partners(parts):
        return [parts[0]] + [exchange(parts[i], chip=i & 1, column=i & 2) for i in range(1, PARTNERS)]

    ids = jnp.concatenate([pair_block, pair_atom], axis=0).reshape(1, -1, LANES)
    ids = jnp.concatenate([ids] + [exchange(ids, chip=chip) for chip in range(1, CHIPS)], axis=0)
    ids = (ids, exchange(ids, core=1))
    rows = to_rows(psi)
    beside = exchange(beta[0], column=1)
    above = exchange(beta[0], chip=2)
    corner = exchange(above, column=1)
    picks = gather(ids, rows)
    shape = (projectors, padded)
    first = jnp.concatenate([after(table, picks[0]) for table in (beta[0], beside)], axis=0)
    picks = partners(picks)
    first = (first, exchange(first, core=1))
    coef = project(ids, first, picks, *shape, 0, ())
    second = jnp.concatenate([after(table, *picks[1:]) for table in (above, corner)], axis=0)
    second = (second, exchange(second, core=1))
    coef = project(ids, second, picks, *shape, 1, (coef,))
    coefs = partners([coef] * PARTNERS)
    count, strength = proj_count.reshape(1, atom_total), strength.transpose(1, 2, 0)
    given = (ids, first + second, count, strength, coefs, *shape)
    results = [None] * PARTNERS
    for wanted in ((2, 3), (1,), (0,)):
        for partner, result in zip(wanted, back_project(wanted, *given)):
            results[partner] = result
    results = partners(results)
    applied = place_rows((0, 2), ids, {0: results[0], 2: results[2]}, psi.shape[1], ())
    return place_rows((1, 3), ids, {1: results[1], 3: results[3]}, psi.shape[1], (applied,))


def plain_project(grid_blocks, tables, atom_ids, block_ids, atom_total):
    picked = jnp.take(grid_blocks, block_ids, axis=1)
    products = jnp.einsum("bkg,kpg->kpb", picked, tables, preferred_element_type=jnp.float32)
    slot_total = products.shape[0]
    onehot = (atom_ids[None, :] == jnp.arange(atom_total, dtype=jnp.int32)[:, None]).astype(
        jnp.float32
    )
    summed = jnp.dot(onehot, products.reshape(slot_total, -1), precision=lax.Precision.HIGHEST)
    return summed.reshape(atom_total, products.shape[1], products.shape[2])


def apply_strength(coef_total, strength, proj_valid):
    masked = coef_total * proj_valid[:, :, None]
    coupled = jnp.einsum("apq,aqb->apb", strength, masked, precision=lax.Precision.HIGHEST)
    return (coupled * proj_valid[:, :, None]).astype(jnp.bfloat16)


def plain_back_project(scaled, tables, atom_ids, block_ids, block_total):
    padded = jnp.concatenate([scaled, jnp.zeros((1,) + scaled.shape[1:], jnp.bfloat16)], axis=0)
    picked = jnp.take(padded, atom_ids, axis=0)
    products = jnp.einsum("kpg,kpb->kbg", tables, picked, preferred_element_type=jnp.float32)
    summed = jax.ops.segment_sum(products, block_ids, num_segments=block_total)
    band_rows = summed.shape[1]
    return summed.transpose(1, 0, 2).reshape(band_rows, -1).astype(jnp.bfloat16)


def plain_body(psi, beta, pair_atom, pair_block, proj_count, strength):
    atom_total = strength.shape[0]
    proj_total = strength.shape[1]
    block_size = beta.shape[2] // proj_total
    proj_valid = (jnp.arange(proj_total, dtype=jnp.int32)[None, :] < proj_count[:, None]).astype(
        jnp.float32
    )
    slab_tables = lax.all_gather(beta, "band", axis=1, tiled=True)
    slot_count = slab_tables.shape[1]
    slab_rows = lax.all_to_all(psi, "slab", split_axis=1, concat_axis=0, tiled=True)
    group_rows = slab_rows.shape[0]
    block_local = slab_rows.shape[1] // block_size
    grid_blocks = slab_rows.reshape(group_rows, block_local, block_size)
    tables = slab_tables.reshape(slot_count, proj_total, block_size)
    atom_ids = pair_atom.reshape(slot_count)
    block_ids = pair_block.reshape(slot_count)
    coef_part = plain_project(grid_blocks, tables, atom_ids, block_ids, atom_total)
    coef_total = lax.psum(coef_part, "slab")
    scaled = apply_strength(coef_total, strength, proj_valid)
    slab_applied = plain_back_project(scaled, tables, atom_ids, block_ids, block_local)
    return lax.all_to_all(slab_applied, "slab", split_axis=0, concat_axis=1, tiled=True)


def solution(mesh):
    placed = (
        P(("band", "slab"), None),
        P("slab", "band", None),
        P("slab", None),
        P("slab", None),
        P(),
        P(),
    )
    columns, slabs = mesh.shape["band"], mesh.shape["slab"]

    def chosen(*args):
        if (columns, slabs) == (PARTNERS, CORES * CHIPS) and args[1].shape[1] % LANES == 0:
            return body(columns, slabs, *args)
        return plain_body(*args)

    return jax.shard_map(
        chosen,
        mesh=mesh,
        in_specs=placed,
        out_specs=P(("band", "slab"), None),
        check_vma=False,
    )
```

```python
import functools

import jax
import jax.numpy as jnp
from jax import lax
from jax.experimental import pallas as pl
from jax.experimental.pallas import tpu as pltpu
from jax.sharding import PartitionSpec as P

CORES = 2
LANES = 128
CHIPS = 4
PARTNERS = 4
PIECES = 4
GROUP = 16
HALVES = 2
GATHER_BYTES = 10_000_000
PROJECT_BYTES = 30_000_000
F32 = jnp.float32
BF16 = jnp.bfloat16
VMEM_SPEC = pl.BlockSpec(memory_space=pltpu.VMEM)
PARAMS = pltpu.CompilerParams(vmem_limit_bytes=40 * 1024 * 1024)


def dot(a, b, contract=((1,), (0,))):
    return lax.dot_general(a, b, (contract, ((), ())), preferred_element_type=F32)


def two_terms(x):
    high = x.astype(BF16)
    return high, (x - high.astype(F32)).astype(BF16)


def after(x, *others):
    return lax.optimization_barrier((x, *others))[0]


def iota(shape, axis):
    return lax.broadcasted_iota(jnp.int32, shape, axis)


def own_place():
    position = lax.axis_index("slab")
    return jnp.bitwise_and(position, CORES - 1), lax.axis_index("band"), jnp.right_shift(position, 1)


def slab_index(place, turned, slab):
    core = place[0] if slab == 0 else CORES - 1 - place[0]
    return jnp.bitwise_xor(place[2], turned) * CORES + core


def owner(turned_chip, turned_column):
    return (turned_chip & 1) | (turned_column & 2), (turned_chip & 2) | (turned_column & 1)


def pieces_of(half_index):
    return range(half_index * PIECES // HALVES, (half_index + 1) * PIECES // HALVES)


def slot_ids(ids_ref, place, turned_chip, turned_column, kind):
    slot_rows = ids_ref.shape[1] // 2
    share = slot_rows // PARTNERS
    first = kind * slot_rows + jnp.bitwise_xor(place[1], turned_column) * share
    return [ids_ref[turned_chip, pl.ds(first + i, 1), :] for i in range(share)]


def atom_hits(ids_ref, place, pieces):
    lane = iota((LANES, LANES), 1)
    for piece in pieces:
        for atoms in slot_ids(ids_ref, place, piece & 2, piece & 1, 1):
            yield (down(atoms) == lane).astype(BF16)


def down(ids):
    return jnp.transpose(jnp.broadcast_to(ids, (LANES, LANES)))


def rows_kernel(psi_ref, out_ref):
    def move(i, carry):
        part = psi_ref[0:1, pl.ds(pl.multiple_of(i * 2048, 2048), 2048)]
        out_ref[pl.ds(pl.multiple_of(i * 16, 16), 16), :] = part.reshape(16, LANES)
        return carry

    lax.fori_loop(0, out_ref.shape[0] // 16, move, 0, unroll=8)


def to_rows(psi):
    rows = psi.shape[1] // LANES
    return pl.pallas_call(
        rows_kernel,
        in_specs=[VMEM_SPEC],
        out_specs=VMEM_SPEC,
        out_shape=jax.ShapeDtypeStruct((rows, LANES), BF16),
        compiler_params=PARAMS,
    )(psi)


def gather_kernel(ids_refs, rows_ref, out_refs):
    half = LANES // 2
    slab_rows = rows_ref.shape[0] // (CORES * CHIPS)
    lane = iota((LANES, LANES), 1)
    low = iota((half, LANES), 1) < half
    for chip in range(CHIPS):
        for slab in range(CORES):
            index = slab_index(own_place(), chip, slab)
            odds, hits, places = [], [], []
            for column in range(PARTNERS):
                partner, piece = owner(chip, column)
                ids = slot_ids(ids_refs[slab], own_place(), chip, column, 0)
                for i, row in enumerate(ids):
                    blocks = down(row)
                    wanted = jnp.right_shift(blocks, 1)
                    odds.append(jnp.bitwise_and(blocks, 1) == 1)
                    hits.append(
                        jnp.concatenate([(wanted - t * LANES == lane).astype(BF16) for t in range(slab_rows // LANES)], axis=1)
                    )
                    places.append((out_refs[partner], ((slab * PIECES + piece) * len(ids) + i) * half))
            first_row = pl.multiple_of(index * slab_rows, slab_rows)
            picked = dot(jnp.concatenate(hits, axis=0), rows_ref[pl.ds(first_row, slab_rows), :])
            for i, (odd, (out_ref, first)) in enumerate(zip(odds, places)):
                straight = picked[i * LANES : (i + 1) * LANES]
                turned = pltpu.roll(straight, half, 1)
                lower = jnp.where(odd, turned, straight)[:half]
                upper = jnp.where(odd, straight, turned)[half:]
                out_ref[first : first + half, :] = jnp.where(low, lower, upper).astype(BF16)


def gather(ids, rows):
    slots = CORES * PIECES * ids[0].shape[1] // 2 * LANES // PARTNERS

    def kernel(own_ids, other_ids, rows_ref, *out_refs):
        gather_kernel((own_ids, other_ids), rows_ref, out_refs)

    return pl.pallas_call(
        kernel,
        in_specs=[VMEM_SPEC] * 3,
        out_specs=[VMEM_SPEC] * PARTNERS,
        out_shape=[jax.ShapeDtypeStruct((slots // 2, LANES), BF16)] * PARTNERS,
        cost_estimate=pl.CostEstimate(flops=0, bytes_accessed=GATHER_BYTES, transcendentals=0),
        compiler_params=PARAMS,
    )(*ids, rows)


def project_kernel(projectors, half_index, ids_refs, table_refs, packed_refs, before_refs, coef_ref, picks_of, terms):
    bands = len(packed_refs)
    slots = table_refs[0].shape[0]
    pair_count = projectors // 2
    wide = 2 * bands * GROUP
    low = iota((bands * GROUP, LANES), 1) < LANES // 2
    folded = (pair_count * wide, bands * projectors)
    gather_lanes = (iota(folded, 0) // GROUP == iota(folded, 1)).astype(BF16)
    diagonal = lax.rem(iota((GROUP, wide), 0), GROUP) == lax.rem(iota((GROUP, wide), 1), GROUP)
    none = jnp.zeros((bands * GROUP, LANES), BF16)
    half = LANES // 2
    left = iota((half, LANES), 1) < half
    for band, packed_ref in enumerate(packed_refs):
        for i in range(CORES * slots // LANES):
            slab, block = divmod(i, slots // LANES)
            first = ((slab * HALVES + half_index) * (slots // LANES) + block) * half
            straight = packed_ref[first : first + half, :].astype(F32)
            turned = pltpu.roll(straight, half, 1)
            picks_of[band, i * LANES : i * LANES + half, :] = jnp.where(left, straight, turned).astype(BF16)
            picks_of[band, i * LANES + half : (i + 1) * LANES, :] = jnp.where(left, turned, straight).astype(BF16)
    of_atom = []
    for slab, table_ref in enumerate(table_refs):
        of_atom += atom_hits(ids_refs[slab], own_place(), pieces_of(half_index))
        for group in range(slots // GROUP):
            rows = slice(group * GROUP, (group + 1) * GROUP)
            first = slab * slots + group * GROUP
            high_rows, rest_rows = slice(first, first + GROUP), slice(CORES * slots + first, CORES * slots + first + GROUP)
            picks = jnp.concatenate([picks_of[band, high_rows, :] for band in range(bands)], axis=0)
            values = jnp.concatenate([jnp.where(low, picks, none), jnp.where(low, none, picks)], axis=0)
            tables = jnp.concatenate([table_ref[rows, t * LANES : (t + 1) * LANES] for t in range(pair_count)], axis=0)
            crossed = dot(tables, values, ((1,), (1,)))
            for t in range(pair_count):
                kept = jnp.where(diagonal, crossed[t * GROUP : (t + 1) * GROUP], 0.0)
                lanes = slice(t * wide, (t + 1) * wide)
                terms[high_rows, lanes], terms[rest_rows, lanes] = two_terms(kept)
    slot_coef = dot(terms[...], gather_lanes)
    high, rest = two_terms(slot_coef[: CORES * slots] + slot_coef[CORES * slots :])
    of_atom = jnp.concatenate(of_atom, axis=0)
    total = dot(high, of_atom, ((0,), (0,))) + dot(rest, of_atom, ((0,), (0,)))
    coef_ref[...] = total + before_refs[0][...] if before_refs else total


def project(ids, tables, picks, projectors, half_index, before):
    bands = len(picks)
    slots = tables[0].shape[0]
    width = projectors * bands * GROUP

    def kernel(own_ids, other_ids, own_ref, other_ref, *rest):
        ends = [bands, bands + len(before)]
        project_kernel(
            projectors, half_index, (own_ids, other_ids), (own_ref, other_ref),
            rest[: ends[0]], rest[ends[0] : ends[1]], *rest[ends[1] :],
        )

    return pl.pallas_call(
        kernel,
        in_specs=[VMEM_SPEC] * (4 + bands + len(before)),
        out_specs=VMEM_SPEC,
        out_shape=jax.ShapeDtypeStruct((bands * projectors, LANES), F32),
        scratch_shapes=[pltpu.VMEM((bands, CORES * slots, LANES), BF16)] + [pltpu.VMEM((2 * CORES * slots, width), BF16)],
        cost_estimate=pl.CostEstimate(flops=0, bytes_accessed=PROJECT_BYTES, transcendentals=0),
        compiler_params=PARAMS,
    )(*ids, *tables, *picks, *before)


def apply_kernel(wanted, projectors, ids_refs, table_refs, count_ref, strength_ref, coef_refs, out_refs, wide_refs):
    pair_count = projectors // 2
    width = projectors * LANES // 2
    atom_total = strength_ref.shape[2]
    half = LANES // 2
    low = iota((half, LANES), 1) < half
    valid = (iota((projectors, atom_total), 0) < count_ref[...]).astype(F32)
    spread = (iota((projectors, width), 0) == iota((projectors, width), 1) // half).astype(BF16)
    for band, wide_ref in zip(wanted, wide_refs):
        coupled = jnp.zeros((projectors, atom_total), F32)
        for q in range(projectors):
            rows = [coef_refs[away][q * PARTNERS + (band ^ away)][None] for away in range(PARTNERS)]
            total = (rows[0] + rows[1] + rows[2] + rows[3]) * valid[q : q + 1]
            coupled = coupled + strength_ref[:, q, :] * total
        scaled = (coupled * valid).astype(BF16)
        wide_ref[...] = dot(scaled, spread, ((0,), (0,))).astype(BF16)
    for slab in range(CORES):
        for half_index in range(HALVES):
            table_ref = table_refs[half_index * CORES + slab]
            blocks = table_ref.shape[0] // LANES
            for i, of_atom in enumerate(atom_hits(ids_refs[slab], own_place(), pieces_of(half_index))):
                rows = slice(i * LANES, (i + 1) * LANES)
                first = ((slab * HALVES + half_index) * blocks + i) * half
                for wide_ref, out_ref in zip(wide_refs, out_refs):
                    total = None
                    for t in range(pair_count):
                        tile = slice(t * LANES, (t + 1) * LANES)
                        term = dot(of_atom, wide_ref[:, tile]) * table_ref[rows, tile].astype(F32)
                        total = term if total is None else total + term
                    total = total + pltpu.roll(total, half, 1)
                    packed = jnp.where(low, total[:half], total[half:])
                    out_ref[first : first + half, :] = packed.astype(BF16)


def back_project(wanted, ids, tables, count, strength, coefs, projectors):
    slots = sum(table.shape[0] for table in tables)
    atom_total = strength.shape[2]

    def kernel(own_ids, other_ids, count_ref, strength_ref, *rest):
        ends = [len(tables), len(tables) + len(coefs), len(tables) + len(coefs) + len(wanted)]
        apply_kernel(
            wanted, projectors, (own_ids, other_ids), rest[: ends[0]], count_ref, strength_ref,
            rest[ends[0] : ends[1]], rest[ends[1] : ends[2]], rest[ends[2] :],
        )

    return pl.pallas_call(
        kernel,
        in_specs=[VMEM_SPEC] * (4 + len(tables) + len(coefs)),
        out_specs=[VMEM_SPEC] * len(wanted),
        out_shape=[jax.ShapeDtypeStruct((slots // 2, LANES), BF16)] * len(wanted),
        scratch_shapes=[pltpu.VMEM((atom_total, projectors * LANES // 2), BF16)] * len(wanted),
        compiler_params=PARAMS,
    )(*ids, count, strength, *tables, *coefs)


def place_kernel(chips, wanted, ids_refs, value_refs, out_ref, stages, sems):
    value_refs = dict(zip(wanted, value_refs))
    core, _, own_chip = place = own_place()
    half = LANES // 2
    points = stages[0].shape[1]
    low = iota((half, LANES), 1) < half
    copies = []
    for chip in chips:
        for slab in range(CORES):
            parts, block_rows = [], []
            for column in range(PARTNERS):
                partner, piece = owner(chip, column)
                ids = slot_ids(ids_refs[slab], place, chip, column, 0)
                for i, blocks in enumerate(ids):
                    block_rows.append(jnp.right_shift(blocks, 1))
                    odd = jnp.bitwise_and(down(blocks), 1) == 1
                    first = ((slab * PIECES + piece) * len(ids) + i) * half
                    value = value_refs[partner][first : first + half, :].astype(F32)
                    turned = pltpu.roll(value, half, 1)
                    odd_a, odd_b = odd[:half], odd[half:]
                    part_a = jnp.where(odd_a, turned, value)
                    part_b = jnp.where(odd_b, value, turned)
                    parts.append(jnp.where(low != odd_a, part_a, 0.0).astype(BF16))
                    parts.append(jnp.where(low != odd_b, part_b, 0.0).astype(BF16))
            values = jnp.concatenate(parts, axis=0)
            block_row = jnp.concatenate(block_rows, axis=1)
            stage = stages[len(copies)]
            for t in range(points // LANES // LANES):
                hits = (iota((LANES, block_row.shape[1]), 0) + t * LANES == block_row).astype(BF16)
                total = dot(hits, values).astype(BF16)
                for i in range(LANES // 16):
                    at = t * LANES * LANES + i * 2048
                    stage[0:1, at : at + 2048] = total[i * 16 : (i + 1) * 16].reshape(1, 2048)
            index = jnp.bitwise_xor(own_chip, chip) * CORES + jnp.bitwise_xor(core, slab)
            there = out_ref.at[:, pl.ds(pl.multiple_of(index * points, points), points)]
            copies.append(pltpu.make_async_copy(stage, there, sems.at[len(copies)]))
            copies[-1].start()
    for copy in copies:
        copy.wait()


def place_rows(chips, ids, values, points, before):
    wanted = tuple(values)
    small = (*ids, *values.values())
    slabs = CORES * len(chips)

    def kernel(*refs):
        first_out = len(small) + len(before)
        stages = refs[first_out + 1 : first_out + 1 + slabs]
        place_kernel(chips, wanted, refs[:CORES], refs[CORES : len(small)], refs[first_out], stages, refs[-1])

    return pl.pallas_call(
        kernel,
        in_specs=[VMEM_SPEC] * len(small) + [pl.BlockSpec(memory_space=pl.ANY)] * len(before),
        out_specs=pl.BlockSpec(memory_space=pl.ANY),
        out_shape=jax.ShapeDtypeStruct((1, points), BF16),
        scratch_shapes=[pltpu.VMEM((1, points // (CORES * CHIPS)), BF16)] * slabs + [pltpu.SemaphoreType.DMA((slabs,))],
        input_output_aliases={len(small): 0} if before else {},
        compiler_params=PARAMS,
    )(*small, *before)


def body(columns, slabs, psi, beta, pair_atom, pair_block, proj_count, strength):
    atom_total, projectors = strength.shape[:2]

    def exchange(x, chip=0, column=0, core=0):
        turned = chip * CORES + core
        if column == 0:
            return lax.ppermute(x, "slab", [(i, i ^ turned) for i in range(slabs)])
        if turned == 0:
            return lax.ppermute(x, "band", [(i, i ^ column) for i in range(columns)])
        pairs = [(i, i ^ (column * slabs + turned)) for i in range(columns * slabs)]
        return lax.ppermute(x, ("band", "slab"), pairs)

    def partners(parts):
        return [parts[0]] + [exchange(parts[i], chip=i & 1, column=i & 2) for i in range(1, PARTNERS)]

    ids = jnp.concatenate([pair_block, pair_atom], axis=0).reshape(1, -1, LANES)
    ids = jnp.concatenate([ids] + [exchange(ids, chip=chip) for chip in range(1, CHIPS)], axis=0)
    ids = (ids, exchange(ids, core=1))
    rows = to_rows(psi)
    beside = exchange(beta[0], column=1)
    above = exchange(beta[0], chip=2)
    corner = exchange(above, column=1)
    picks = gather(ids, rows)
    first = jnp.concatenate([after(table, picks[0]) for table in (beta[0], beside)], axis=0)
    picks = partners(picks)
    first = (first, exchange(first, core=1))
    coef = project(ids, first, picks, projectors, 0, ())
    second = jnp.concatenate([after(table, *picks[1:]) for table in (above, corner)], axis=0)
    second = (second, exchange(second, core=1))
    coef = project(ids, second, picks, projectors, 1, (coef,))
    coefs = partners([coef] * PARTNERS)
    count, strength = proj_count.reshape(1, atom_total), strength.transpose(1, 2, 0)
    given = (ids, first + second, count, strength, coefs, projectors)
    results = [None] * PARTNERS
    for wanted in ((2, 3), (1,), (0,)):
        for partner, result in zip(wanted, back_project(wanted, *given)):
            results[partner] = result
    results = partners(results)
    applied = place_rows((0, 2), ids, {0: results[0], 2: results[2]}, psi.shape[1], ())
    return place_rows((1, 3), ids, {1: results[1], 3: results[3]}, psi.shape[1], (applied,))


def plain_project(grid_blocks, tables, atom_ids, block_ids, atom_total):
    picked = jnp.take(grid_blocks, block_ids, axis=1)
    products = jnp.einsum("bkg,kpg->kpb", picked, tables, preferred_element_type=jnp.float32)
    slot_total = products.shape[0]
    onehot = (atom_ids[None, :] == jnp.arange(atom_total, dtype=jnp.int32)[:, None]).astype(
        jnp.float32
    )
    summed = jnp.dot(onehot, products.reshape(slot_total, -1), precision=lax.Precision.HIGHEST)
    return summed.reshape(atom_total, products.shape[1], products.shape[2])


def apply_strength(coef_total, strength, proj_valid):
    masked = coef_total * proj_valid[:, :, None]
    coupled = jnp.einsum("apq,aqb->apb", strength, masked, precision=lax.Precision.HIGHEST)
    return (coupled * proj_valid[:, :, None]).astype(jnp.bfloat16)


def plain_back_project(scaled, tables, atom_ids, block_ids, block_total):
    padded = jnp.concatenate([scaled, jnp.zeros((1,) + scaled.shape[1:], jnp.bfloat16)], axis=0)
    picked = jnp.take(padded, atom_ids, axis=0)
    products = jnp.einsum("kpg,kpb->kbg", tables, picked, preferred_element_type=jnp.float32)
    summed = jax.ops.segment_sum(products, block_ids, num_segments=block_total)
    band_rows = summed.shape[1]
    return summed.transpose(1, 0, 2).reshape(band_rows, -1).astype(jnp.bfloat16)


def plain_body(psi, beta, pair_atom, pair_block, proj_count, strength):
    atom_total = strength.shape[0]
    proj_total = strength.shape[1]
    block_size = beta.shape[2] // proj_total
    proj_valid = (jnp.arange(proj_total, dtype=jnp.int32)[None, :] < proj_count[:, None]).astype(
        jnp.float32
    )
    slab_tables = lax.all_gather(beta, "band", axis=1, tiled=True)
    slot_count = slab_tables.shape[1]
    slab_rows = lax.all_to_all(psi, "slab", split_axis=1, concat_axis=0, tiled=True)
    group_rows = slab_rows.shape[0]
    block_local = slab_rows.shape[1] // block_size
    grid_blocks = slab_rows.reshape(group_rows, block_local, block_size)
    tables = slab_tables.reshape(slot_count, proj_total, block_size)
    atom_ids = pair_atom.reshape(slot_count)
    block_ids = pair_block.reshape(slot_count)
    coef_part = plain_project(grid_blocks, tables, atom_ids, block_ids, atom_total)
    coef_total = lax.psum(coef_part, "slab")
    scaled = apply_strength(coef_total, strength, proj_valid)
    slab_applied = plain_back_project(scaled, tables, atom_ids, block_ids, block_local)
    return lax.all_to_all(slab_applied, "slab", split_axis=0, concat_axis=1, tiled=True)


def solution(mesh):
    placed = (
        P(("band", "slab"), None),
        P("slab", "band", None),
        P("slab", None),
        P("slab", None),
        P(),
        P(),
    )
    columns, slabs = mesh.shape["band"], mesh.shape["slab"]

    def chosen(*args):
        if (columns, slabs) == (PARTNERS, CORES * CHIPS) and args[1].shape[1] % LANES == 0:
            return body(columns, slabs, *args)
        return plain_body(*args)

    return jax.shard_map(
        chosen,
        mesh=mesh,
        in_specs=placed,
        out_specs=P(("band", "slab"), None),
        check_vma=False,
    )
```

```python
import functools

import jax
import jax.numpy as jnp
from jax import lax
from jax.experimental import pallas as pl
from jax.experimental.pallas import tpu as pltpu
from jax.sharding import PartitionSpec as P

CORES = 2
LANES = 128
CHIPS = 4
PARTNERS = 4
PIECES = 4
GROUP = 16
HALVES = 2
GATHER_BYTES = 10_000_000
PROJECT_BYTES = 30_000_000
F32 = jnp.float32
BF16 = jnp.bfloat16
VMEM_SPEC = pl.BlockSpec(memory_space=pltpu.VMEM)
PARAMS = pltpu.CompilerParams(vmem_limit_bytes=40 * 1024 * 1024)


def dot(a, b, contract=((1,), (0,))):
    return lax.dot_general(a, b, (contract, ((), ())), preferred_element_type=F32)


def same(number, wanted):
    near = number.astype(F32).astype(BF16) == wanted.astype(F32).astype(BF16)
    return jnp.where(near, jnp.ones((), BF16), jnp.zeros((), BF16))


def two_terms(x):
    high = x.astype(BF16)
    return high, (x - high.astype(F32)).astype(BF16)


def after(x, *others):
    return lax.optimization_barrier((x, *others))[0]


def iota(shape, axis):
    return lax.broadcasted_iota(jnp.int32, shape, axis)


def own_place():
    position = lax.axis_index("slab")
    return jnp.bitwise_and(position, CORES - 1), lax.axis_index("band"), jnp.right_shift(position, 1)


def slab_index(place, turned, slab):
    core = place[0] if slab == 0 else CORES - 1 - place[0]
    return jnp.bitwise_xor(place[2], turned) * CORES + core


def owner(turned_chip, turned_column):
    return (turned_chip & 1) | (turned_column & 2), (turned_chip & 2) | (turned_column & 1)


def pieces_of(half_index):
    return range(half_index * PIECES // HALVES, (half_index + 1) * PIECES // HALVES)


def slot_ids(ids_ref, place, turned_chip, turned_column, kind):
    slot_rows = ids_ref.shape[1] // 2
    share = slot_rows // PARTNERS
    first = kind * slot_rows + jnp.bitwise_xor(place[1], turned_column) * share
    return [ids_ref[turned_chip, pl.ds(first + i, 1), :] for i in range(share)]


def atom_hits(ids_ref, place, pieces):
    lane = iota((LANES, LANES), 1)
    for piece in pieces:
        for atoms in slot_ids(ids_ref, place, piece & 2, piece & 1, 1):
            yield (down(atoms) == lane).astype(BF16)


def down(ids):
    return jnp.transpose(jnp.broadcast_to(ids, (LANES, LANES)))


def rows_kernel(psi_ref, out_ref):
    def move(i, carry):
        part = psi_ref[0:1, pl.ds(pl.multiple_of(i * 2048, 2048), 2048)]
        out_ref[pl.ds(pl.multiple_of(i * 16, 16), 16), :] = part.reshape(16, LANES)
        return carry

    lax.fori_loop(0, out_ref.shape[0] // 16, move, 0, unroll=8)


def to_rows(psi):
    rows = psi.shape[1] // LANES
    return pl.pallas_call(
        rows_kernel,
        in_specs=[VMEM_SPEC],
        out_specs=VMEM_SPEC,
        out_shape=jax.ShapeDtypeStruct((rows, LANES), BF16),
        compiler_params=PARAMS,
    )(psi)


def gather_kernel(ids_refs, rows_ref, out_refs):
    half = LANES // 2
    slab_rows = rows_ref.shape[0] // (CORES * CHIPS)
    lane = iota((LANES, LANES), 1)
    low = iota((half, LANES), 1) < half
    for chip in range(CHIPS):
        for slab in range(CORES):
            index = slab_index(own_place(), chip, slab)
            odds, hits, places = [], [], []
            for column in range(PARTNERS):
                partner, piece = owner(chip, column)
                ids = slot_ids(ids_refs[slab], own_place(), chip, column, 0)
                for i, row in enumerate(ids):
                    blocks = down(row)
                    wanted = jnp.right_shift(blocks, 1)
                    odds.append(jnp.bitwise_and(blocks, 1) == 1)
                    hits.append(
                        jnp.concatenate([(wanted - t * LANES == lane).astype(BF16) for t in range(slab_rows // LANES)], axis=1)
                    )
                    places.append((out_refs[partner], ((slab * PIECES + piece) * len(ids) + i) * half))
            first_row = pl.multiple_of(index * slab_rows, slab_rows)
            picked = dot(jnp.concatenate(hits, axis=0), rows_ref[pl.ds(first_row, slab_rows), :])
            for i, (odd, (out_ref, first)) in enumerate(zip(odds, places)):
                straight = picked[i * LANES : (i + 1) * LANES]
                turned = pltpu.roll(straight, half, 1)
                lower = jnp.where(odd, turned, straight)[:half]
                upper = jnp.where(odd, straight, turned)[half:]
                out_ref[first : first + half, :] = jnp.where(low, lower, upper).astype(BF16)


def gather(ids, rows):
    slots = CORES * PIECES * ids[0].shape[1] // 2 * LANES // PARTNERS

    def kernel(own_ids, other_ids, rows_ref, *out_refs):
        gather_kernel((own_ids, other_ids), rows_ref, out_refs)

    return pl.pallas_call(
        kernel,
        in_specs=[VMEM_SPEC] * 3,
        out_specs=[VMEM_SPEC] * PARTNERS,
        out_shape=[jax.ShapeDtypeStruct((slots // 2, LANES), BF16)] * PARTNERS,
        cost_estimate=pl.CostEstimate(flops=0, bytes_accessed=GATHER_BYTES, transcendentals=0),
        compiler_params=PARAMS,
    )(*ids, rows)


def project_kernel(projectors, half_index, ids_refs, table_refs, packed_refs, before_refs, coef_ref, picks_of, terms):
    bands = len(packed_refs)
    slots = table_refs[0].shape[0]
    pair_count = projectors // 2
    wide = 2 * bands * GROUP
    low = iota((bands * GROUP, LANES), 1) < LANES // 2
    folded = (pair_count * wide, bands * projectors)
    gather_lanes = (iota(folded, 0) // GROUP == iota(folded, 1)).astype(BF16)
    diagonal = lax.rem(iota((GROUP, wide), 0), GROUP) == lax.rem(iota((GROUP, wide), 1), GROUP)
    none = jnp.zeros((bands * GROUP, LANES), BF16)
    half = LANES // 2
    left = iota((half, LANES), 1) < half
    for band, packed_ref in enumerate(packed_refs):
        for i in range(CORES * slots // LANES):
            slab, block = divmod(i, slots // LANES)
            first = ((slab * HALVES + half_index) * (slots // LANES) + block) * half
            straight = packed_ref[first : first + half, :].astype(F32)
            turned = pltpu.roll(straight, half, 1)
            picks_of[band, i * LANES : i * LANES + half, :] = jnp.where(left, straight, turned).astype(BF16)
            picks_of[band, i * LANES + half : (i + 1) * LANES, :] = jnp.where(left, turned, straight).astype(BF16)
    of_atom = []
    for slab, table_ref in enumerate(table_refs):
        of_atom += atom_hits(ids_refs[slab], own_place(), pieces_of(half_index))
        for group in range(slots // GROUP):
            rows = slice(group * GROUP, (group + 1) * GROUP)
            first = slab * slots + group * GROUP
            high_rows, rest_rows = slice(first, first + GROUP), slice(CORES * slots + first, CORES * slots + first + GROUP)
            picks = jnp.concatenate([picks_of[band, high_rows, :] for band in range(bands)], axis=0)
            values = jnp.concatenate([jnp.where(low, picks, none), jnp.where(low, none, picks)], axis=0)
            tables = jnp.concatenate([table_ref[rows, t * LANES : (t + 1) * LANES] for t in range(pair_count)], axis=0)
            crossed = dot(tables, values, ((1,), (1,)))
            for t in range(pair_count):
                kept = jnp.where(diagonal, crossed[t * GROUP : (t + 1) * GROUP], 0.0)
                lanes = slice(t * wide, (t + 1) * wide)
                terms[high_rows, lanes], terms[rest_rows, lanes] = two_terms(kept)
    slot_coef = dot(terms[...], gather_lanes)
    high, rest = two_terms(slot_coef[: CORES * slots] + slot_coef[CORES * slots :])
    of_atom = jnp.concatenate(of_atom, axis=0)
    total = dot(high, of_atom, ((0,), (0,))) + dot(rest, of_atom, ((0,), (0,)))
    coef_ref[...] = total + before_refs[0][...] if before_refs else total


def project(ids, tables, picks, projectors, half_index, before):
    bands = len(picks)
    slots = tables[0].shape[0]
    width = projectors * bands * GROUP

    def kernel(own_ids, other_ids, own_ref, other_ref, *rest):
        ends = [bands, bands + len(before)]
        project_kernel(
            projectors, half_index, (own_ids, other_ids), (own_ref, other_ref),
            rest[: ends[0]], rest[ends[0] : ends[1]], *rest[ends[1] :],
        )

    return pl.pallas_call(
        kernel,
        in_specs=[VMEM_SPEC] * (4 + bands + len(before)),
        out_specs=VMEM_SPEC,
        out_shape=jax.ShapeDtypeStruct((bands * projectors, LANES), F32),
        scratch_shapes=[pltpu.VMEM((bands, CORES * slots, LANES), BF16)] + [pltpu.VMEM((2 * CORES * slots, width), BF16)],
        cost_estimate=pl.CostEstimate(flops=0, bytes_accessed=PROJECT_BYTES, transcendentals=0),
        compiler_params=PARAMS,
    )(*ids, *tables, *picks, *before)


def apply_kernel(wanted, projectors, ids_refs, table_refs, count_ref, strength_ref, coef_refs, out_refs, wide_refs):
    pair_count = projectors // 2
    width = projectors * LANES // 2
    atom_total = strength_ref.shape[2]
    half = LANES // 2
    low = iota((half, LANES), 1) < half
    valid = (iota((projectors, atom_total), 0) < count_ref[...]).astype(F32)
    spread = (iota((projectors, width), 0) == iota((projectors, width), 1) // half).astype(BF16)
    for band, wide_ref in zip(wanted, wide_refs):
        coupled = jnp.zeros((projectors, atom_total), F32)
        for q in range(projectors):
            rows = [coef_refs[away][q * PARTNERS + (band ^ away)][None] for away in range(PARTNERS)]
            total = (rows[0] + rows[1] + rows[2] + rows[3]) * valid[q : q + 1]
            coupled = coupled + strength_ref[:, q, :] * total
        scaled = (coupled * valid).astype(BF16)
        wide_ref[...] = dot(scaled, spread, ((0,), (0,))).astype(BF16)
    for slab in range(CORES):
        for half_index in range(HALVES):
            table_ref = table_refs[half_index * CORES + slab]
            blocks = table_ref.shape[0] // LANES
            for i, of_atom in enumerate(atom_hits(ids_refs[slab], own_place(), pieces_of(half_index))):
                rows = slice(i * LANES, (i + 1) * LANES)
                first = ((slab * HALVES + half_index) * blocks + i) * half
                for wide_ref, out_ref in zip(wide_refs, out_refs):
                    total = None
                    for t in range(pair_count):
                        tile = slice(t * LANES, (t + 1) * LANES)
                        term = dot(of_atom, wide_ref[:, tile]) * table_ref[rows, tile].astype(F32)
                        total = term if total is None else total + term
                    total = total + pltpu.roll(total, half, 1)
                    packed = jnp.where(low, total[:half], total[half:])
                    out_ref[first : first + half, :] = packed.astype(BF16)


def back_project(wanted, ids, tables, count, strength, coefs, projectors):
    slots = sum(table.shape[0] for table in tables)
    atom_total = strength.shape[2]

    def kernel(own_ids, other_ids, count_ref, strength_ref, *rest):
        ends = [len(tables), len(tables) + len(coefs), len(tables) + len(coefs) + len(wanted)]
        apply_kernel(
            wanted, projectors, (own_ids, other_ids), rest[: ends[0]], count_ref, strength_ref,
            rest[ends[0] : ends[1]], rest[ends[1] : ends[2]], rest[ends[2] :],
        )

    return pl.pallas_call(
        kernel,
        in_specs=[VMEM_SPEC] * (4 + len(tables) + len(coefs)),
        out_specs=[VMEM_SPEC] * len(wanted),
        out_shape=[jax.ShapeDtypeStruct((slots // 2, LANES), BF16)] * len(wanted),
        scratch_shapes=[pltpu.VMEM((atom_total, projectors * LANES // 2), BF16)] * len(wanted),
        compiler_params=PARAMS,
    )(*ids, count, strength, *tables, *coefs)


def place_kernel(chips, wanted, ids_refs, value_refs, out_ref, stages, sems):
    value_refs = dict(zip(wanted, value_refs))
    core, _, own_chip = place = own_place()
    half = LANES // 2
    points = stages[0].shape[1]
    low = iota((half, LANES), 1) < half
    copies = []
    for chip in chips:
        for slab in range(CORES):
            parts, block_rows = [], []
            for column in range(PARTNERS):
                partner, piece = owner(chip, column)
                ids = slot_ids(ids_refs[slab], place, chip, column, 0)
                for i, blocks in enumerate(ids):
                    block_rows.append(jnp.right_shift(blocks, 1))
                    odd = jnp.bitwise_and(down(blocks), 1) == 1
                    first = ((slab * PIECES + piece) * len(ids) + i) * half
                    value = value_refs[partner][first : first + half, :].astype(F32)
                    turned = pltpu.roll(value, half, 1)
                    odd_a, odd_b = odd[:half], odd[half:]
                    part_a = jnp.where(odd_a, turned, value)
                    part_b = jnp.where(odd_b, value, turned)
                    parts.append(jnp.where(low != odd_a, part_a, 0.0).astype(BF16))
                    parts.append(jnp.where(low != odd_b, part_b, 0.0).astype(BF16))
            values = jnp.concatenate(parts, axis=0)
            block_row = jnp.concatenate(block_rows, axis=1)
            stage = stages[len(copies)]
            number = iota((LANES, block_row.shape[1]), 0)
            for t in range(points // LANES // LANES):
                hits = same(number, block_row - t * LANES)
                total = dot(hits, values).astype(BF16)
                for i in range(LANES // 16):
                    at = t * LANES * LANES + i * 2048
                    stage[0:1, at : at + 2048] = total[i * 16 : (i + 1) * 16].reshape(1, 2048)
            index = jnp.bitwise_xor(own_chip, chip) * CORES + jnp.bitwise_xor(core, slab)
            there = out_ref.at[:, pl.ds(pl.multiple_of(index * points, points), points)]
            copies.append(pltpu.make_async_copy(stage, there, sems.at[len(copies)]))
            copies[-1].start()
    for copy in copies:
        copy.wait()


def place_rows(chips, ids, values, points, before):
    wanted = tuple(values)
    small = (*ids, *values.values())
    slabs = CORES * len(chips)

    def kernel(*refs):
        first_out = len(small) + len(before)
        stages = refs[first_out + 1 : first_out + 1 + slabs]
        place_kernel(chips, wanted, refs[:CORES], refs[CORES : len(small)], refs[first_out], stages, refs[-1])

    return pl.pallas_call(
        kernel,
        in_specs=[VMEM_SPEC] * len(small) + [pl.BlockSpec(memory_space=pl.ANY)] * len(before),
        out_specs=pl.BlockSpec(memory_space=pl.ANY),
        out_shape=jax.ShapeDtypeStruct((1, points), BF16),
        scratch_shapes=[pltpu.VMEM((1, points // (CORES * CHIPS)), BF16)] * slabs + [pltpu.SemaphoreType.DMA((slabs,))],
        input_output_aliases={len(small): 0} if before else {},
        compiler_params=PARAMS,
    )(*small, *before)


def body(columns, slabs, psi, beta, pair_atom, pair_block, proj_count, strength):
    atom_total, projectors = strength.shape[:2]

    def exchange(x, chip=0, column=0, core=0):
        turned = chip * CORES + core
        if column == 0:
            return lax.ppermute(x, "slab", [(i, i ^ turned) for i in range(slabs)])
        if turned == 0:
            return lax.ppermute(x, "band", [(i, i ^ column) for i in range(columns)])
        pairs = [(i, i ^ (column * slabs + turned)) for i in range(columns * slabs)]
        return lax.ppermute(x, ("band", "slab"), pairs)

    def partners(parts):
        return [parts[0]] + [exchange(parts[i], chip=i & 1, column=i & 2) for i in range(1, PARTNERS)]

    ids = jnp.concatenate([pair_block, pair_atom], axis=0).reshape(1, -1, LANES)
    ids = jnp.concatenate([ids] + [exchange(ids, chip=chip) for chip in range(1, CHIPS)], axis=0)
    ids = (ids, exchange(ids, core=1))
    rows = to_rows(psi)
    beside = exchange(beta[0], column=1)
    above = exchange(beta[0], chip=2)
    corner = exchange(above, column=1)
    picks = gather(ids, rows)
    first = jnp.concatenate([after(table, picks[0]) for table in (beta[0], beside)], axis=0)
    picks = partners(picks)
    first = (first, exchange(first, core=1))
    coef = project(ids, first, picks, projectors, 0, ())
    second = jnp.concatenate([after(table, *picks[1:]) for table in (above, corner)], axis=0)
    second = (second, exchange(second, core=1))
    coef = project(ids, second, picks, projectors, 1, (coef,))
    coefs = partners([coef] * PARTNERS)
    count, strength = proj_count.reshape(1, atom_total), strength.transpose(1, 2, 0)
    given = (ids, first + second, count, strength, coefs, projectors)
    results = [None] * PARTNERS
    for wanted in ((2, 3), (1,), (0,)):
        for partner, result in zip(wanted, back_project(wanted, *given)):
            results[partner] = result
    results = partners(results)
    applied = place_rows((0, 2), ids, {0: results[0], 2: results[2]}, psi.shape[1], ())
    return place_rows((1, 3), ids, {1: results[1], 3: results[3]}, psi.shape[1], (applied,))


def plain_project(grid_blocks, tables, atom_ids, block_ids, atom_total):
    picked = jnp.take(grid_blocks, block_ids, axis=1)
    products = jnp.einsum("bkg,kpg->kpb", picked, tables, preferred_element_type=jnp.float32)
    slot_total = products.shape[0]
    onehot = (atom_ids[None, :] == jnp.arange(atom_total, dtype=jnp.int32)[:, None]).astype(
        jnp.float32
    )
    summed = jnp.dot(onehot, products.reshape(slot_total, -1), precision=lax.Precision.HIGHEST)
    return summed.reshape(atom_total, products.shape[1], products.shape[2])


def apply_strength(coef_total, strength, proj_valid):
    masked = coef_total * proj_valid[:, :, None]
    coupled = jnp.einsum("apq,aqb->apb", strength, masked, precision=lax.Precision.HIGHEST)
    return (coupled * proj_valid[:, :, None]).astype(jnp.bfloat16)


def plain_back_project(scaled, tables, atom_ids, block_ids, block_total):
    padded = jnp.concatenate([scaled, jnp.zeros((1,) + scaled.shape[1:], jnp.bfloat16)], axis=0)
    picked = jnp.take(padded, atom_ids, axis=0)
    products = jnp.einsum("kpg,kpb->kbg", tables, picked, preferred_element_type=jnp.float32)
    summed = jax.ops.segment_sum(products, block_ids, num_segments=block_total)
    band_rows = summed.shape[1]
    return summed.transpose(1, 0, 2).reshape(band_rows, -1).astype(jnp.bfloat16)


def plain_body(psi, beta, pair_atom, pair_block, proj_count, strength):
    atom_total = strength.shape[0]
    proj_total = strength.shape[1]
    block_size = beta.shape[2] // proj_total
    proj_valid = (jnp.arange(proj_total, dtype=jnp.int32)[None, :] < proj_count[:, None]).astype(
        jnp.float32
    )
    slab_tables = lax.all_gather(beta, "band", axis=1, tiled=True)
    slot_count = slab_tables.shape[1]
    slab_rows = lax.all_to_all(psi, "slab", split_axis=1, concat_axis=0, tiled=True)
    group_rows = slab_rows.shape[0]
    block_local = slab_rows.shape[1] // block_size
    grid_blocks = slab_rows.reshape(group_rows, block_local, block_size)
    tables = slab_tables.reshape(slot_count, proj_total, block_size)
    atom_ids = pair_atom.reshape(slot_count)
    block_ids = pair_block.reshape(slot_count)
    coef_part = plain_project(grid_blocks, tables, atom_ids, block_ids, atom_total)
    coef_total = lax.psum(coef_part, "slab")
    scaled = apply_strength(coef_total, strength, proj_valid)
    slab_applied = plain_back_project(scaled, tables, atom_ids, block_ids, block_local)
    return lax.all_to_all(slab_applied, "slab", split_axis=0, concat_axis=1, tiled=True)


def solution(mesh):
    placed = (
        P(("band", "slab"), None),
        P("slab", "band", None),
        P("slab", None),
        P("slab", None),
        P(),
        P(),
    )
    columns, slabs = mesh.shape["band"], mesh.shape["slab"]

    def chosen(*args):
        if (columns, slabs) == (PARTNERS, CORES * CHIPS) and args[1].shape[1] % LANES == 0:
            return body(columns, slabs, *args)
        return plain_body(*args)

    return jax.shard_map(
        chosen,
        mesh=mesh,
        in_specs=placed,
        out_specs=P(("band", "slab"), None),
        check_vma=False,
    )
```
